512 devices in a mesh: group: 4 (over z_lo), expert: 128 (over y, z_hi, x, core).
Axes of the slice: x: 4, y: 8, z: 8 (z_hi: 2, z_lo: 4; z = z_hi * 4 + z_lo), core: 2. Of those that a mesh axis runs over, the one named last changes fastest.
Arguments:
- master_weights: float32 [128, 2048, 384], P('group', 'expert'), may hold values from -0.125 to 0.125
- first_moment: float32 [128, 2048, 384], P('group', 'expert'), may hold values from -3 to 3
- second_moment: float32 [128, 2048, 384], P('group', 'expert'), may hold values from 1 to 16
- gradient: bfloat16 [128, 2048, 384], P('group', 'expert'), may hold values from -24 to 24
- placement: int32 [4, 128], replicated, may hold values from 0 to 127, each once within a row
- tokens: bfloat16 [4, 512, 2048], P('group', 'expert'), may hold values from -6 to 6
- routed_expert_index: int32 [4, 512, 8], P('group', 'expert'), may hold values from 0 to 15, all different within a row; in each aligned block of 4 rows (0 to 3, 4 to 7, ..., all dimensions but the last counted through in order) at most 3 rows name the same one
- gate_weights: float32 [4, 512, 8], P('group', 'expert'), may hold values from 0.2 to 1
Outputs:
- master_out: float32 [128, 2048, 384], P('group', 'expert')
- rollout_weights: bfloat16 [4, 128, 2048, 384], P('group', 'expert')
- decoded: bfloat16 [4, 512, 2048], P('group', 'expert')
The draws below stay inside these ranges and needn't reach their ends.
Inputs may be any that keep to these rules, and one draw needn't show every extreme that they name: Each row of placement is a permutation; entry u names the device of that group that holds slab u, hidden units (u % 8) * 128 onward of expert u // 8. `routed_expert_index`: each row names 8 different experts. Among the rows of one device no expert is named by more than 3 rows, and in every draw some device has an expert named by exactly 3 rows.
All inputs are finite; a program needn't handle non-finite values.
Results may differ from the reference program's by a relative error of at most 0.0055.
The reference program's roundings to bfloat16 on the way count: a program that leaves them out, or rounds other values in their place, can miss the bound.
Values may be sent and summed in bfloat16 or wider, within the bound.
No kernel may reach another device: no remote copies, remote signals or barrier semaphores. Data moves between devices by JAX's collectives and lax.ppermute only.
A program may use at most 64 MiB of HBM per device.

```python
import math
import jax
import jax.numpy as jnp
import numpy as np
from jax import lax

D = 2048
FFW = 1024
ROWS_DEV = 4
FF_DEV = 128
EXPERTS = 16
TOPK = 8
MOST = 3
ROWS = 512
N_GROUP = 4
N_EXPERT = 128


def block_scale(own_key, dims, shards, least, largest):
    def one(dim, blocks):
        heights = jax.random.uniform(jax.random.fold_in(jax.random.fold_in(own_key, 6), dim), (blocks,), jnp.float32, least / len(shards), largest / len(shards))
        return jnp.repeat(jnp.exp(heights), dims[dim] // blocks).reshape((-1,) + (1,) * (len(dims) - dim - 1))

    loudness = one(*shards[0])
    for cut in shards[1:]:
        loudness = loudness * one(*cut)
    return loudness


def shared_out(own_key, own, number, rows, amount, top, bound, skew):
    ranking = jax.random.permutation(own_key, amount)
    packed, ordinary = load_shares(amount, rows * top, bound, skew, True), load_shares(amount, rows * top, bound, skew, False)
    places = jnp.arange(amount)

    def named(lengths, turn):
        used = int((lengths > 0).sum())
        fixed = max(1, used // 4)
        moved = fixed + (places - fixed + turn * (used - fixed)) % max(1, amount - fixed)
        return jnp.zeros((amount,), jnp.int32).at[ranking[jnp.where(places < fixed, places, moved)]].set(jnp.asarray(lengths, jnp.int32))

    lengths = jnp.where(number % 4 == 0, named(packed, number // 4), named(ordinary, number - number // 4 - 1))
    mixed = jax.random.permutation(jax.random.fold_in(own, 3), amount)
    giver, taker = mixed[0:amount // 2 * 2:2], mixed[1:amount // 2 * 2:2]
    margin = jnp.minimum(lengths[giver] - 1, bound - lengths[taker]) // 2
    margin = jnp.where((giver == ranking[0]) | (taker == ranking[0]) | (lengths[taker] == 0), 0, jnp.maximum(margin, 0))
    moved = jax.random.randint(jax.random.fold_in(own, 4), (amount // 2,), 0, 1 << 20) % (margin + 1)
    lengths = lengths.at[giver].add(-moved).at[taker].add(moved)
    items = jnp.searchsorted(jnp.cumsum(lengths), jnp.arange(rows * top), side="right").astype(jnp.int32)
    grid = items.reshape(top, rows).T
    grid = grid[jax.random.permutation(jax.random.fold_in(own, 1), rows)]
    turn = jax.random.randint(jax.random.fold_in(own, 2), (rows, 1), 0, top)
    return jnp.take_along_axis(grid, (jnp.arange(top)[None, :] + turn) % top, axis=1)


def load_shares(count, total, limit, skew, full):
    portions = [(1 << 20) // math.isqrt(grade ** skew) + 1 for grade in range(1, count + 1)]
    largest = limit if full else min(limit, max(-(-total // count), total * portions[0] // sum(portions)))
    least = 1 if total - largest >= count - 1 else 0
    given, spare = [largest] + [least] * (count - 1), total - largest - least * (count - 1)
    while spare > 0:
        free = [i for i in range(1, count) if given[i] < largest] or [i for i in range(1, count) if given[i] < limit]
        pool, budget = sum([portions[i] for i in free]), spare
        for i in free:
            more = min(limit - given[i], max(1, budget * portions[i] // pool), spare)
            given[i] = given[i] + more
            spare = spare - more
    return np.array(given)


def centred(stream_key, extent, width, bound, pieces=(), kind=jnp.bfloat16):
    drawn = jax.random.normal(stream_key, extent, jnp.float32) * width
    if len(pieces) > 0:
        drawn = block_scale(stream_key, extent, pieces, -0.22, 0.18) * drawn
    return jnp.clip(drawn, min=-bound, max=bound).astype(kind)


def setup_inputs(seed: int = 0) -> dict:
    seeds = jax.random.split(jax.random.key(seed), 9)
    master_weights = centred(seeds[0], (N_EXPERT, D, 3 * FF_DEV), D ** -0.5, 0.125, ((0, 4), (1, 128)), jnp.float32)
    first_moment = centred(seeds[1], (N_EXPERT, D, 3 * FF_DEV), 0.5, 3.0, ((0, 4), (1, 128)), jnp.float32)
    second_moment = jnp.clip(jnp.exp(math.log(16.0) - 2.7725887 * jax.random.uniform(seeds[2], (N_EXPERT, D, 3 * FF_DEV), jnp.float32) ** block_scale(seeds[2], (N_EXPERT, D, 3 * FF_DEV), ((0, 4), (1, 128)), -0.2, 0.2)), 1.0, 16.0)
    gradient = centred(seeds[3], (N_EXPERT, D, 3 * FF_DEV), 4.0, 24.0, ((0, 4), (1, 128)))
    placement = jax.vmap(lambda own: jax.random.permutation(own, N_EXPERT))(jax.random.split(seeds[4], N_GROUP)).reshape((N_GROUP, N_EXPERT)).astype(jnp.int32)
    tokens = centred(seeds[5], (N_GROUP, ROWS, D), 1.0, 6.0, ((0, 4), (1, 128)))
    routed_expert_index_keys = jax.random.split(jax.random.fold_in(seeds[6], 1), N_GROUP * ROWS // ROWS_DEV)
    routed_expert_index_turns = jax.random.permutation(jax.random.fold_in(seeds[6], 3), N_GROUP * ROWS // ROWS_DEV)
    routed_expert_index = jax.vmap(lambda own, number: shared_out(jax.random.fold_in(seeds[6], 2), own, number, ROWS_DEV, EXPERTS, TOPK, MOST, 2))(routed_expert_index_keys, routed_expert_index_turns).reshape((N_GROUP, ROWS, TOPK))
    gate_weights = jnp.clip(0.2 + 0.8 * jax.random.uniform(seeds[7], (N_GROUP, ROWS, TOPK), jnp.float32) ** block_scale(seeds[7], (N_GROUP, ROWS, TOPK), ((0, 4), (1, 128)), -0.2, 0.2), 0.2, 1.0)
    return {"master_weights": master_weights, "first_moment": first_moment, "second_moment": second_moment, "gradient": gradient, "placement": placement, "tokens": tokens, "routed_expert_index": routed_expert_index, "gate_weights": gate_weights}


adam_step = 1000.0
adam_eps = 1e-08
learn_rate = 0.005
weight_decay = 0.1
beta_one = 0.9
beta_two = 0.999

def reference(master_weights, first_moment, second_moment, gradient, placement, tokens, routed_expert_index, gate_weights):
    grad_float = gradient.astype(jnp.float32)
    first_new = beta_one * first_moment + (1.0 - beta_one) * grad_float
    second_new = beta_two * second_moment + (1.0 - beta_two) * grad_float * grad_float
    update = first_new / (1.0 - beta_one ** adam_step) / (jnp.sqrt(second_new / (1.0 - beta_two ** adam_step)) + adam_eps)
    master_out = master_weights - learn_rate * (update + weight_decay * master_weights)
    rounded_down_value = master_out.astype(jnp.bfloat16)
    unit_ids = jnp.arange(N_EXPERT, dtype=jnp.int32)
    matches = placement[:, :, None] == unit_ids[None, None, :]
    holders = lax.optimization_barrier(jnp.sum(jnp.where(matches, unit_ids[None, :, None], 0), axis=1)).astype(jnp.int32)
    rollout = jnp.take(rounded_down_value, holders, axis=0)
    slab_count = FFW // FF_DEV
    blocks = rounded_down_value.reshape(EXPERTS, slab_count, D, 3 * FF_DEV)
    expert_index_span = jnp.arange(EXPERTS, dtype=jnp.int32)
    decoded_all = []
    for group_index in range(N_GROUP):
        inputs = tokens[group_index].astype(jnp.float32)
        onehot = routed_expert_index[group_index][:, :, None] == expert_index_span[None, None, :]
        coefficient = lax.optimization_barrier(jnp.sum(jnp.where(onehot, gate_weights[group_index][:, :, None], 0.0), axis=1))

        def expert_step(running, operand):
            expert_block, column_gate = operand
            block_float = expert_block.astype(jnp.float32)
            gate_up = jnp.einsum('rd,sdf->srf', inputs, block_float[:, :, :2 * FF_DEV])
            hidden = (jax.nn.silu(gate_up[..., :FF_DEV]) * gate_up[..., FF_DEV:]).astype(jnp.bfloat16)
            hidden = lax.optimization_barrier(hidden).astype(jnp.float32)
            partial_value = jnp.einsum('srf,sdf->srd', hidden, block_float[:, :, 2 * FF_DEV:]).astype(jnp.bfloat16)
            partial_value = lax.optimization_barrier(partial_value).astype(jnp.float32)
            return (running + column_gate[:, None] * lax.optimization_barrier(jnp.sum(partial_value, axis=0)), None)
        running, _ = lax.scan(expert_step, jnp.zeros((ROWS, D), jnp.float32), (blocks, coefficient.T))
        decoded_all.append(running.astype(jnp.bfloat16))
    return (master_out, rollout, jnp.stack(decoded_all))
```

```python
import jax
import jax.numpy as jnp
from jax import lax
from jax.experimental import pallas as pl
from jax.experimental.pallas import tpu as pltpu
from jax.sharding import Mesh, PartitionSpec as P

adam_step = 1000.0
adam_eps = 1e-08
learn_rate = 0.005
weight_decay = 0.1
beta_one = 0.9
beta_two = 0.999

GROUPS, YS, ZHS, XS, CORES = 4, 8, 2, 4, 2
ALONG = ("y", "zh", "x", "c")
EXPERT_COUNT = 16
EXTRA = 128


def pick_slabs(order, parts):
    count, rows, cols = parts[0].shape
    total = count * len(parts)

    def kernel(order_ref, a, b, c, d, out_ref, held, sems):
        copies = [
            pltpu.make_async_copy(ref, held.at[pl.ds(k * count, count)], sems.at[k])
            for k, ref in enumerate((a, b, c, d))
        ]
        for copy in copies:
            copy.start()
        for copy in copies:
            copy.wait()

        def body(i, _):
            out_ref[i] = held[order_ref[i]]
            return 0

        lax.fori_loop(0, total, body, 0, unroll=8)

    return pl.pallas_call(
        kernel,
        out_shape=jax.ShapeDtypeStruct((total, rows, cols), parts[0].dtype),
        in_specs=[pl.BlockSpec(memory_space=pltpu.SMEM)] + [pl.BlockSpec(memory_space=pl.ANY)] * 4,
        out_specs=pl.BlockSpec(memory_space=pltpu.VMEM),
        scratch_shapes=[
            pltpu.VMEM((total, rows, cols), parts[0].dtype),
            pltpu.SemaphoreType.DMA((4,)),
        ],
        compiler_params=pltpu.CompilerParams(vmem_limit_bytes=16 * 2**20),
    )(order, *parts)


def hidden_and_down(expert_id, rows_ext, weights):
    row_count = rows_ext.shape[0]
    depth = weights.shape[0]
    plane = XS * CORES
    piece = depth // plane

    def kernel(expert_ref, rows_ref, w_ref, out_ref):
        gate_up = jnp.dot(
            rows_ref[:, :depth], w_ref[:, :256], preferred_element_type=jnp.float32
        )
        gate, up = gate_up[:, :128], gate_up[:, 128:]
        hidden = (gate / (1.0 + jnp.exp(-gate)) * up).astype(jnp.bfloat16).astype(jnp.float32)
        lane = lax.broadcasted_iota(jnp.int32, (row_count, EXTRA), 1)
        own = (lane == expert_ref[0]) | (lane == expert_ref[0] + EXPERT_COUNT)
        extra = rows_ref[:, depth:].astype(jnp.float32)
        coefficient = jnp.sum(jnp.where(own, extra, 0.0), axis=1, keepdims=True)
        scaled = (hidden * coefficient).astype(jnp.bfloat16)
        for k in range(plane):
            out_ref[k, :row_count, :] = scaled
            out_ref[k, row_count:, :] = w_ref[k * piece : (k + 1) * piece, 256:]

    return pl.pallas_call(
        kernel,
        out_shape=jax.ShapeDtypeStruct((plane, row_count + piece, 128), jnp.bfloat16),
        in_specs=[pl.BlockSpec(memory_space=pltpu.SMEM)] + [pl.BlockSpec(memory_space=pltpu.VMEM)] * 2,
        out_specs=pl.BlockSpec(memory_space=pltpu.VMEM),
        compiler_params=pltpu.CompilerParams(vmem_limit_bytes=32 * 2**20),
    )(expert_id, rows_ext, weights)


def down_sum(blocks, row_count):
    plane, both, width = blocks.shape
    piece = both - row_count

    def kernel(ref, out_ref):
        total = jnp.zeros((row_count, piece), jnp.float32)
        for k in range(plane):
            total += lax.dot_general(
                ref[k, :row_count, :],
                ref[k, row_count:, :],
                (((1,), (1,)), ((), ())),
                preferred_element_type=jnp.float32,
            )
        out_ref[...] = total.astype(jnp.bfloat16)

    return pl.pallas_call(
        kernel,
        out_shape=jax.ShapeDtypeStruct((row_count, piece), jnp.bfloat16),
        in_specs=[pl.BlockSpec(memory_space=pltpu.VMEM)],
        out_specs=pl.BlockSpec(memory_space=pltpu.VMEM),
        compiler_params=pltpu.CompilerParams(vmem_limit_bytes=32 * 2**20),
    )(blocks)


def per_device(
    master_weights,
    first_moment,
    second_moment,
    gradient,
    placement,
    tokens,
    routed_expert_index,
    gate_weights,
):
    group = lax.axis_index("g")
    place = lax.axis_index(ALONG)
    row_count, depth = tokens.shape[1:]

    experts = jnp.arange(EXPERT_COUNT, dtype=jnp.int32)
    named = routed_expert_index[0][:, :, None] == experts[None, None, :]
    coefficient = jnp.sum(jnp.where(named, gate_weights[0][:, :, None], 0.0), axis=1)
    high = coefficient.astype(jnp.bfloat16)
    low = (coefficient - high.astype(jnp.float32)).astype(jnp.bfloat16)
    fill = jnp.zeros((row_count, EXTRA - 2 * EXPERT_COUNT), jnp.bfloat16)
    own_rows = jnp.concatenate([tokens[0], high, low, fill], axis=1)
    spread = jnp.broadcast_to(own_rows[None], (YS * ZHS,) + own_rows.shape)
    some_rows = lax.all_to_all(spread, ("y", "zh"), split_axis=0, concat_axis=0, tiled=True)
    all_rows = lax.all_gather(some_rows, ("x", "c"), axis=0, tiled=False)
    all_rows = all_rows.transpose(1, 0, 2, 3).reshape(-1, depth + EXTRA)

    grad_float = gradient.astype(jnp.float32)
    first_new = beta_one * first_moment + (1.0 - beta_one) * grad_float
    second_new = beta_two * second_moment + (1.0 - beta_two) * grad_float * grad_float
    update = (
        first_new
        / (1.0 - beta_one**adam_step)
        / (jnp.sqrt(second_new / (1.0 - beta_two**adam_step)) + adam_eps)
    )
    master_out = master_weights - learn_rate * (update + weight_decay * master_weights)
    rounded = master_out.astype(jnp.bfloat16)

    parts = [rounded] + [
        lax.ppermute(rounded, "g", [(i, (i + s) % GROUPS) for i in range(GROUPS)])
        for s in range(1, GROUPS)
    ]
    unit_count = placement.shape[1]
    per_group = unit_count // GROUPS
    unit_ids = jnp.arange(unit_count, dtype=jnp.int32)
    own_row = lax.dynamic_index_in_dim(placement, group, 0, keepdims=False)
    matches = own_row[:, None] == unit_ids[None, :]
    holder = jnp.sum(jnp.where(matches, unit_ids[:, None], 0), axis=0)
    order = ((group - holder // per_group) % GROUPS) * per_group + holder % per_group
    ordered = pick_slabs(order, parts)
    own_slab = lax.all_to_all(ordered, ALONG, split_axis=0, concat_axis=0, tiled=True)
    weights = own_slab.reshape(depth, -1)
    rollout_out = weights[None, None]

    slabs_each = unit_count // EXPERT_COUNT
    expert_id = jnp.sum(jnp.where(unit_ids == place, holder, 0), keepdims=True) // slabs_each
    blocks = hidden_and_down(expert_id, all_rows, weights)
    blocks = lax.all_to_all(blocks, ("x", "c"), split_axis=0, concat_axis=0, tiled=True)
    partial = down_sum(blocks, all_rows.shape[0])
    piece = partial.shape[1]
    lanes = piece // 128
    chunks = partial.reshape(unit_count, row_count, lanes, 128).transpose(0, 2, 1, 3)
    chunks = chunks.reshape(unit_count, lanes * row_count, 128)
    returned = lax.all_to_all(chunks, ALONG, split_axis=0, concat_axis=0, tiled=True)
    returned = returned.reshape(YS * ZHS, XS * CORES, lanes, row_count, 128)
    decoded = jnp.sum(returned.astype(jnp.float32), axis=0)
    decoded = decoded.transpose(2, 0, 1, 3).reshape(1, row_count, depth)
    return (master_out, rollout_out, decoded.astype(jnp.bfloat16))


def solution(mesh):
    names = ("g",) + ALONG
    fine = Mesh(mesh.devices.reshape(GROUPS, YS, ZHS, XS, CORES), names)
    split = P("g", ALONG, None)
    return jax.shard_map(
        per_device,
        mesh=fine,
        in_specs=(split, split, split, split, P(), split, split, split),
        out_specs=(split, P("g", ALONG, None, None), split),
        check_vma=False,
    )
```

```python
import jax
import jax.numpy as jnp
from jax import lax
from jax.experimental import pallas as pl
from jax.experimental.pallas import tpu as pltpu
from jax.sharding import Mesh, PartitionSpec as P

adam_step = 1000.0
adam_eps = 1e-08
learn_rate = 0.005
weight_decay = 0.1
beta_one = 0.9
beta_two = 0.999

GROUPS, YS, ZHS, XS, CORES = 4, 8, 2, 4, 2
ALONG = ("y", "zh", "x", "c")
EXPERT_COUNT = 16
EXTRA = 128


def place_slabs(places, parts):
    count, rows, cols = parts[0].shape
    total = count * len(parts)

    def kernel(places_ref, a, b, c, d, out_ref):
        for k, ref in enumerate((a, b, c, d)):

            def body(i, _, k=k, ref=ref):
                out_ref[places_ref[k * count + i]] = ref[i]
                return 0

            lax.fori_loop(0, count, body, 0, unroll=8)

    return pl.pallas_call(
        kernel,
        out_shape=jax.ShapeDtypeStruct((total, rows, cols), parts[0].dtype),
        in_specs=[pl.BlockSpec(memory_space=pltpu.SMEM)] + [pl.BlockSpec(memory_space=pltpu.VMEM)] * 4,
        out_specs=pl.BlockSpec(memory_space=pltpu.VMEM),
        compiler_params=pltpu.CompilerParams(vmem_limit_bytes=16 * 2**20),
    )(places, *parts)


def hidden_units(numbers, rows_ext, weights):
    row_count = rows_ext.shape[0]
    depth, cols = weights.shape
    half = row_count // CORES
    blocks = 4
    block = row_count // blocks

    def kernel(numbers_ref, rows_hbm, w_ref, send_ref, keep_ref, slab_hbm, rows_ref, scaled_ref, row_sems, slab_sem):
        copies = [
            pltpu.make_async_copy(
                rows_hbm.at[pl.ds(k * block, block)], rows_ref.at[pl.ds(k * block, block)], row_sems.at[k]
            )
            for k in range(blocks)
        ]
        for copy in copies:
            copy.start()
        slab_copy = pltpu.make_async_copy(w_ref, slab_hbm, slab_sem)
        slab_copy.start()
        send_ref[half:, :] = w_ref[:, 256:]
        expert = numbers_ref[0]
        core = numbers_ref[1]
        for k in range(blocks):
            copies[k].wait()
            span = slice(k * block, (k + 1) * block)
            gate_up = jnp.dot(
                rows_ref[span, :depth], w_ref[:, :256], preferred_element_type=jnp.float32
            )
            gate, up = gate_up[:, :128], gate_up[:, 128:]
            hidden = (gate / (1.0 + jnp.exp(-gate)) * up).astype(jnp.bfloat16).astype(jnp.float32)
            lane = lax.broadcasted_iota(jnp.int32, (block, EXTRA), 1)
            own = (lane == expert) | (lane == expert + EXPERT_COUNT)
            extra = rows_ref[span, depth:].astype(jnp.float32)
            coefficient = jnp.sum(jnp.where(own, extra, 0.0), axis=1, keepdims=True)
            scaled_ref[span, :] = (hidden * coefficient).astype(jnp.bfloat16)
        at = lax.broadcasted_iota(jnp.int32, (half, row_count), 0)
        of = lax.broadcasted_iota(jnp.int32, (half, row_count), 1)
        each, column = row_count // (XS * CORES * YS * ZHS), YS * ZHS
        row = at % each
        x = at // each % XS
        y_zh = at // (each * XS)
        base = x * CORES * column * each + y_zh * each + row

        def rows_of(k):
            pick = jnp.where(of == base + k * (column * each), 1.0, 0.0).astype(jnp.bfloat16)
            return jnp.dot(pick, scaled_ref[...], preferred_element_type=jnp.float32).astype(jnp.bfloat16)

        send_ref[:half, :] = rows_of(1 - core)
        keep_ref[...] = rows_of(core)
        slab_copy.wait()

    return pl.pallas_call(
        kernel,
        out_shape=(
            jax.ShapeDtypeStruct((half + depth, 128), jnp.bfloat16),
            jax.ShapeDtypeStruct((half, 128), jnp.bfloat16),
            jax.ShapeDtypeStruct((depth, cols), jnp.bfloat16),
        ),
        in_specs=[
            pl.BlockSpec(memory_space=pltpu.SMEM),
            pl.BlockSpec(memory_space=pltpu.HBM),
            pl.BlockSpec(memory_space=pltpu.VMEM),
        ],
        out_specs=(
            pl.BlockSpec(memory_space=pltpu.VMEM),
            pl.BlockSpec(memory_space=pltpu.VMEM),
            pl.BlockSpec(memory_space=pltpu.HBM),
        ),
        scratch_shapes=[
            pltpu.VMEM(rows_ext.shape, jnp.bfloat16),
            pltpu.VMEM((row_count, 128), jnp.bfloat16),
            pltpu.SemaphoreType.DMA((blocks,)),
            pltpu.SemaphoreType.DMA,
        ],
        compiler_params=pltpu.CompilerParams(vmem_limit_bytes=52 * 2**20),
    )(numbers, rows_ext, weights)


def pair_outputs(keep, weights, received):
    half = keep.shape[0]
    depth = weights.shape[0]
    chips = half // 4
    lanes = depth // 128

    def kernel(keep_ref, w_ref, recv_ref, out_ref, part_ref):
        across = (((1,), (1,)), ((), ()))
        for k in range(4):
            span = slice(k * depth // 4, (k + 1) * depth // 4)
            part_ref[:, span] = lax.dot_general(
                keep_ref[...], w_ref[span, 256:], across, preferred_element_type=jnp.float32
            ) + lax.dot_general(
                recv_ref[:half, :],
                recv_ref[half + span.start : half + span.stop, :],
                across,
                preferred_element_type=jnp.float32,
            )
        low = lax.broadcasted_iota(jnp.int32, (chips // 2, 8, 128), 1) < 4

        def tile(q):
            return part_ref[:, q * 128 : (q + 1) * 128].reshape(chips // 2, 8, 128)

        for q in range(0, lanes, 4):
            first, second = [], []
            for p in (q, q + 2):
                a, b = tile(p), tile(p + 1)
                first.append(jnp.where(low, a, pltpu.roll(b, 4, 1)))
                second.append(jnp.where(low, pltpu.roll(a, 4, 1), b))
            out_ref[:, 0, 4 * q : 4 * q + 16, :] = jnp.concatenate(first, axis=1).astype(jnp.bfloat16)
            out_ref[:, 1, 4 * q : 4 * q + 16, :] = jnp.concatenate(second, axis=1).astype(jnp.bfloat16)

    out = pl.pallas_call(
        kernel,
        out_shape=jax.ShapeDtypeStruct((chips // 2, 2, 4 * lanes, 128), jnp.bfloat16),
        in_specs=[pl.BlockSpec(memory_space=pltpu.VMEM)] * 3,
        out_specs=pl.BlockSpec(memory_space=pltpu.VMEM),
        scratch_shapes=[pltpu.VMEM((half, depth), jnp.float32)],
        compiler_params=pltpu.CompilerParams(vmem_limit_bytes=32 * 2**20),
    )(keep, weights, received)
    return out.reshape(chips, 4 * lanes, 128)


def sum_chunks(chunks):
    count, tall, _ = chunks.shape
    lanes = tall // 4

    def kernel(ref, out_ref):
        total = ref[0].astype(jnp.float32)
        for k in range(1, count):
            total += ref[k].astype(jnp.float32)
        out_ref[...] = jnp.concatenate(
            [total[4 * q : 4 * q + 4, :] for q in range(lanes)], axis=1
        ).astype(jnp.bfloat16)

    return pl.pallas_call(
        kernel,
        out_shape=jax.ShapeDtypeStruct((4, lanes * 128), jnp.bfloat16),
        in_specs=[pl.BlockSpec(memory_space=pltpu.VMEM)],
        out_specs=pl.BlockSpec(memory_space=pltpu.VMEM),
        compiler_params=pltpu.CompilerParams(vmem_limit_bytes=32 * 2**20),
    )(chunks)


def per_device(
    master_weights,
    first_moment,
    second_moment,
    gradient,
    placement,
    tokens,
    routed_expert_index,
    gate_weights,
):
    group = lax.axis_index("g")
    core = lax.axis_index("c")
    place = lax.axis_index(ALONG)
    row_count, depth = tokens.shape[1:]

    grad_float = gradient.astype(jnp.float32)
    first_new = beta_one * first_moment + (1.0 - beta_one) * grad_float
    second_new = beta_two * second_moment + (1.0 - beta_two) * grad_float * grad_float
    update = (
        first_new
        / (1.0 - beta_one**adam_step)
        / (jnp.sqrt(second_new / (1.0 - beta_two**adam_step)) + adam_eps)
    )
    master_out = master_weights - learn_rate * (update + weight_decay * master_weights)
    rounded = master_out.astype(jnp.bfloat16)

    experts = jnp.arange(EXPERT_COUNT, dtype=jnp.int32)
    named = routed_expert_index[0][:, :, None] == experts[None, None, :]
    coefficient = jnp.sum(jnp.where(named, gate_weights[0][:, :, None], 0.0), axis=1)
    high = coefficient.astype(jnp.bfloat16)
    low = (coefficient - high.astype(jnp.float32)).astype(jnp.bfloat16)
    fill = jnp.zeros((row_count, EXTRA - 2 * EXPERT_COUNT), jnp.bfloat16)
    own_rows = jnp.concatenate([tokens[0], high, low, fill], axis=1)
    spread = jnp.broadcast_to(own_rows[None], (YS * ZHS,) + own_rows.shape)
    rounded, spread = lax.optimization_barrier((rounded, spread))

    parts = [rounded] + [
        lax.ppermute(rounded, "g", [(i, (i + s) % GROUPS) for i in range(GROUPS)])
        for s in range(1, GROUPS)
    ]
    some_rows = lax.all_to_all(spread, ("y", "zh"), split_axis=0, concat_axis=0, tiled=True)
    some_rows = some_rows.reshape(-1, depth + EXTRA)
    parts, _ = lax.optimization_barrier((parts, some_rows))

    unit_count = placement.shape[1]
    unit_ids = jnp.arange(unit_count, dtype=jnp.int32)
    own_row = lax.dynamic_index_in_dim(placement, group, 0, keepdims=False)
    by_group = own_row.reshape(GROUPS, -1)
    places = jnp.take(by_group, (group - jnp.arange(GROUPS)) % GROUPS, axis=0).reshape(-1)
    ordered = place_slabs(places, parts)
    own_slab = lax.all_to_all(ordered, ALONG, split_axis=0, concat_axis=0, tiled=True)
    weights = own_slab.reshape(depth, -1)

    all_rows = lax.all_gather(some_rows, ("x", "c"), axis=0, tiled=True)

    slabs_each = unit_count // EXPERT_COUNT
    expert_id = jnp.sum(jnp.where(own_row == place, unit_ids, 0)) // slabs_each
    numbers = jnp.stack([expert_id, core]).astype(jnp.int32)
    send, keep, slab = hidden_units(numbers, all_rows, weights)
    received = lax.ppermute(send, "c", [(0, 1), (1, 0)])
    chunks = pair_outputs(keep, weights, received)
    chunks = lax.all_to_all(chunks, ("y", "zh", "x"), split_axis=0, concat_axis=0, tiled=True)
    decoded = sum_chunks(chunks)
    return (master_out, slab[None, None], decoded[None])


def solution(mesh):
    names = ("g",) + ALONG
    fine = Mesh(mesh.devices.reshape(GROUPS, YS, ZHS, XS, CORES), names)
    split = P("g", ALONG, None)
    return jax.shard_map(
        per_device,
        mesh=fine,
        in_specs=(split, split, split, split, P(), split, split, split),
        out_specs=(split, P("g", ALONG, None, None), split),
        check_vma=False,
    )
```

```python
import jax
import jax.numpy as jnp
from jax import lax
from jax.experimental import pallas as pl
from jax.experimental.pallas import tpu as pltpu
from jax.sharding import Mesh, PartitionSpec as P

adam_step = 1000.0
adam_eps = 1e-08
learn_rate = 0.005
weight_decay = 0.1
beta_one = 0.9
beta_two = 0.999

GROUPS, YS, ZHS, XS, CORES = 4, 8, 2, 4, 2
ALONG = ("y", "zh", "x", "c")
EXPERT_COUNT = 16
EXTRA = 128


def place_slabs(places, parts):
    count, rows, cols = parts[0].shape
    total = count * len(parts)

    def kernel(places_ref, a, b, c, d, out_ref):
        for k, ref in enumerate((a, b, c, d)):

            def body(i, _, k=k, ref=ref):
                out_ref[places_ref[k * count + i]] = ref[i]
                return 0

            lax.fori_loop(0, count, body, 0, unroll=8)

    return pl.pallas_call(
        kernel,
        out_shape=jax.ShapeDtypeStruct((total, rows, cols), parts[0].dtype),
        in_specs=[pl.BlockSpec(memory_space=pltpu.SMEM)] + [pl.BlockSpec(memory_space=pltpu.VMEM)] * 4,
        out_specs=pl.BlockSpec(memory_space=pltpu.VMEM),
        compiler_params=pltpu.CompilerParams(vmem_limit_bytes=16 * 2**20),
    )(places, *parts)


def hidden_units(numbers, rows_ext, weights):
    row_count = rows_ext.shape[0]
    depth = weights.shape[0]
    half = row_count // CORES

    def kernel(numbers_ref, rows_hbm, w_hbm, send_ref, keep_ref, slab_hbm, rows_ref, w_ref, scaled_ref, sems):
        copies = [
            pltpu.make_async_copy(w_hbm, w_ref, sems.at[0]),
            pltpu.make_async_copy(rows_hbm, rows_ref, sems.at[1]),
        ]
        for copy in copies:
            copy.start()
        expert = numbers_ref[0]
        core = numbers_ref[1]
        at = lax.broadcasted_iota(jnp.int32, (half, row_count), 0)
        of = lax.broadcasted_iota(jnp.int32, (half, row_count), 1)
        each, column = row_count // (XS * CORES * YS * ZHS), YS * ZHS
        row = at % each
        x = at // each % XS
        y_zh = at // (each * XS)
        away = of - (x * CORES * column * each + y_zh * each + row)
        lane = lax.broadcasted_iota(jnp.int32, (row_count, EXTRA), 1)
        own = (lane == expert) | (lane == expert + EXPERT_COUNT)
        for copy in copies:
            copy.wait()
        slab_copy = pltpu.make_async_copy(w_ref, slab_hbm, sems.at[2])
        slab_copy.start()
        gate_up = jnp.dot(
            rows_ref[:, :depth], w_ref[:, :256], preferred_element_type=jnp.float32
        )
        gate, up = gate_up[:, :128], gate_up[:, 128:]
        hidden = (gate / (1.0 + jnp.exp(-gate)) * up).astype(jnp.bfloat16).astype(jnp.float32)
        extra = rows_ref[:, depth:].astype(jnp.float32)
        coefficient = jnp.sum(jnp.where(own, extra, 0.0), axis=1, keepdims=True)
        scaled_ref[...] = (hidden * coefficient).astype(jnp.bfloat16)
        send_ref[half:, :] = w_ref[:, 256:]
        keep_ref[half:, :] = w_ref[:, 256:]

        def rows_of(k):
            pick = jnp.where(away == k * (column * each), 1.0, 0.0).astype(jnp.bfloat16)
            return jnp.dot(pick, scaled_ref[...], preferred_element_type=jnp.float32).astype(jnp.bfloat16)

        send_ref[:half, :] = rows_of(1 - core)
        keep_ref[:half, :] = rows_of(core)
        slab_copy.wait()

    return pl.pallas_call(
        kernel,
        out_shape=(jax.ShapeDtypeStruct((half + depth, 128), jnp.bfloat16),) * 2
        + (jax.ShapeDtypeStruct(weights.shape, jnp.bfloat16),),
        in_specs=[
            pl.BlockSpec(memory_space=pltpu.SMEM),
            pl.BlockSpec(memory_space=pltpu.HBM),
            pl.BlockSpec(memory_space=pltpu.HBM),
        ],
        out_specs=(pl.BlockSpec(memory_space=pltpu.VMEM),) * 2 + (pl.BlockSpec(memory_space=pltpu.HBM),),
        scratch_shapes=[
            pltpu.VMEM(rows_ext.shape, jnp.bfloat16),
            pltpu.VMEM(weights.shape, jnp.bfloat16),
            pltpu.VMEM((row_count, 128), jnp.bfloat16),
            pltpu.SemaphoreType.DMA((3,)),
        ],
        compiler_params=pltpu.CompilerParams(vmem_limit_bytes=52 * 2**20),
    )(numbers, rows_ext, weights)


def pair_outputs(kept, received):
    chips = YS * ZHS * XS
    half = chips * 4
    depth = kept.shape[0] - half
    lanes = depth // 128

    def kernel(kept_ref, recv_ref, out_ref, part_ref):
        for k in range(4):
            span = slice(half + k * depth // 4, half + (k + 1) * depth // 4)
            part_ref[:, k * depth // 4 : (k + 1) * depth // 4] = sum(
                lax.dot_general(
                    ref[:half, :], ref[span, :], (((1,), (1,)), ((), ())), preferred_element_type=jnp.float32
                )
                for ref in (kept_ref, recv_ref)
            )
        low = lax.broadcasted_iota(jnp.int32, (chips // 2, 8, 128), 1) < 4

        def tile(q):
            return part_ref[:, q * 128 : (q + 1) * 128].reshape(chips // 2, 8, 128)

        for q in range(0, lanes, 4):
            first, second = [], []
            for p in (q, q + 2):
                a, b = tile(p), tile(p + 1)
                first.append(jnp.where(low, a, pltpu.roll(b, 4, 1)))
                second.append(jnp.where(low, pltpu.roll(a, 4, 1), b))
            out_ref[:, 0, 4 * q : 4 * q + 16, :] = jnp.concatenate(first, axis=1).astype(jnp.bfloat16)
            out_ref[:, 1, 4 * q : 4 * q + 16, :] = jnp.concatenate(second, axis=1).astype(jnp.bfloat16)

    out = pl.pallas_call(
        kernel,
        out_shape=jax.ShapeDtypeStruct((chips // 2, 2, 4 * lanes, 128), jnp.bfloat16),
        in_specs=[pl.BlockSpec(memory_space=pltpu.VMEM)] * 2,
        out_specs=pl.BlockSpec(memory_space=pltpu.VMEM),
        scratch_shapes=[pltpu.VMEM((half, depth), jnp.float32)],
        compiler_params=pltpu.CompilerParams(vmem_limit_bytes=24 * 2**20),
    )(kept, received)
    return out.reshape(chips, 4 * lanes, 128)


def sum_chunks(chunks):
    count, tall, _ = chunks.shape
    lanes = tall // 4

    def kernel(ref, out_ref):
        total = ref[0].astype(jnp.float32)
        for k in range(1, count):
            total += ref[k].astype(jnp.float32)
        out_ref[...] = jnp.concatenate(
            [total[4 * q : 4 * q + 4, :] for q in range(lanes)], axis=1
        ).astype(jnp.bfloat16)

    return pl.pallas_call(
        kernel,
        out_shape=jax.ShapeDtypeStruct((4, lanes * 128), jnp.bfloat16),
        in_specs=[pl.BlockSpec(memory_space=pltpu.VMEM)],
        out_specs=pl.BlockSpec(memory_space=pltpu.VMEM),
        compiler_params=pltpu.CompilerParams(vmem_limit_bytes=32 * 2**20),
    )(chunks)


def per_device(
    master_weights,
    first_moment,
    second_moment,
    gradient,
    placement,
    tokens,
    routed_expert_index,
    gate_weights,
):
    group = lax.axis_index("g")
    core = lax.axis_index("c")
    place = lax.axis_index(ALONG)
    row_count, depth = tokens.shape[1:]

    grad_float = gradient.astype(jnp.float32)
    first_new = beta_one * first_moment + (1.0 - beta_one) * grad_float
    second_new = beta_two * second_moment + (1.0 - beta_two) * grad_float * grad_float
    update = (
        first_new
        / (1.0 - beta_one**adam_step)
        / (jnp.sqrt(second_new / (1.0 - beta_two**adam_step)) + adam_eps)
    )
    master_out = master_weights - learn_rate * (update + weight_decay * master_weights)
    rounded = master_out.astype(jnp.bfloat16)

    parts = [rounded] + [
        lax.ppermute(rounded, "g", [(i, (i + s) % GROUPS) for i in range(GROUPS)])
        for s in range(1, GROUPS)
    ]

    parts[1], tokens, routed_expert_index, gate_weights = lax.optimization_barrier(
        (parts[1], tokens, routed_expert_index, gate_weights)
    )
    experts = jnp.arange(EXPERT_COUNT, dtype=jnp.int32)
    named = routed_expert_index[0][:, :, None] == experts[None, None, :]
    coefficient = jnp.sum(jnp.where(named, gate_weights[0][:, :, None], 0.0), axis=1)
    high = coefficient.astype(jnp.bfloat16)
    low = (coefficient - high.astype(jnp.float32)).astype(jnp.bfloat16)
    fill = jnp.zeros((row_count, EXTRA - 2 * EXPERT_COUNT), jnp.bfloat16)
    own_rows = jnp.concatenate([tokens[0], high, low, fill], axis=1)
    spread = jnp.broadcast_to(own_rows[None], (YS * ZHS,) + own_rows.shape)
    some_rows = lax.all_to_all(spread, ("y", "zh"), split_axis=0, concat_axis=0, tiled=True)
    some_rows = some_rows.reshape(-1, depth + EXTRA)
    parts, _ = lax.optimization_barrier((parts, some_rows))

    unit_count = placement.shape[1]
    unit_ids = jnp.arange(unit_count, dtype=jnp.int32)
    own_row = lax.dynamic_index_in_dim(placement, group, 0, keepdims=False)
    by_group = own_row.reshape(GROUPS, -1)
    places = jnp.take(by_group, (group - jnp.arange(GROUPS)) % GROUPS, axis=0).reshape(-1)
    ordered = place_slabs(places, parts)
    own_slab = lax.all_to_all(ordered, ALONG, split_axis=0, concat_axis=0, tiled=True)
    weights = own_slab.reshape(depth, -1)

    all_rows = lax.all_gather(some_rows, ("x", "c"), axis=0, tiled=True)

    slabs_each = unit_count // EXPERT_COUNT
    expert_id = jnp.sum(jnp.where(own_row == place, unit_ids, 0)) // slabs_each
    numbers = jnp.stack([expert_id, core]).astype(jnp.int32)
    sent, kept, slab = hidden_units(numbers, all_rows, weights)
    received = lax.ppermute(sent, "c", [(0, 1), (1, 0)])
    chunks = pair_outputs(kept, received)
    chunks = lax.all_to_all(chunks, ("y", "zh", "x"), split_axis=0, concat_axis=0, tiled=True)
    decoded = sum_chunks(chunks)
    return (master_out, slab[None, None], decoded[None])


def solution(mesh):
    names = ("g",) + ALONG
    fine = Mesh(mesh.devices.reshape(GROUPS, YS, ZHS, XS, CORES), names)
    split = P("g", ALONG, None)
    return jax.shard_map(
        per_device,
        mesh=fine,
        in_specs=(split, split, split, split, P(), split, split, split),
        out_specs=(split, P("g", ALONG, None, None), split),
        check_vma=False,
    )
```

```python
import jax
import jax.numpy as jnp
from jax import lax
from jax.experimental import pallas as pl
from jax.experimental.pallas import tpu as pltpu
from jax.sharding import Mesh, PartitionSpec as P

adam_step = 1000.0
adam_eps = 1e-08
learn_rate = 0.005
weight_decay = 0.1
beta_one = 0.9
beta_two = 0.999

GROUPS, YS, ZHS, XS, CORES = 4, 8, 2, 4, 2
ALONG = ("y", "zh", "x", "c")
EXPERT_COUNT = 16
EXTRA = 128
ROOM = 32


def place_slabs(places, parts):
    count, rows, cols = parts[0].shape
    total = count * len(parts)

    def kernel(places_ref, a, b, c, d, out_ref):
        for k, ref in enumerate((a, b, c, d)):

            def body(i, _, k=k, ref=ref):
                out_ref[places_ref[k * count + i]] = ref[i]
                return 0

            lax.fori_loop(0, count, body, 0, unroll=8)

    return pl.pallas_call(
        kernel,
        out_shape=jax.ShapeDtypeStruct((total, rows, cols), parts[0].dtype),
        in_specs=[pl.BlockSpec(memory_space=pltpu.SMEM)] + [pl.BlockSpec(memory_space=pltpu.VMEM)] * 4,
        out_specs=pl.BlockSpec(memory_space=pltpu.VMEM),
        compiler_params=pltpu.CompilerParams(vmem_limit_bytes=16 * 2**20),
    )(places, *parts)


def hidden_units(expert_id, pick, rows_ext, weights):
    row_count = rows_ext.shape[0]
    depth = weights.shape[0]
    half = row_count // CORES

    def kernel(expert_ref, pick_ref, rows_hbm, w_ref, send_ref, keep_ref, slab_hbm, rows_ref, scaled_ref, sems):
        rows_copy = pltpu.make_async_copy(rows_hbm, rows_ref, sems.at[0])
        rows_copy.start()
        slab_copy = pltpu.make_async_copy(w_ref, slab_hbm, sems.at[1])
        slab_copy.start()
        send_ref[half:, :] = w_ref[:, 256:]
        keep_ref[half:, :] = w_ref[:, 256:]
        expert = expert_ref[0]
        lane = lax.broadcasted_iota(jnp.int32, (1, EXTRA), 1)
        own = jnp.where((lane == expert) | (lane == expert + EXPERT_COUNT), 1.0, 0.0)
        rows_copy.wait()
        gate_up = jnp.dot(
            rows_ref[:, :depth], w_ref[:, :256], preferred_element_type=jnp.float32
        )
        gate, up = gate_up[:, :128], gate_up[:, 128:]
        hidden = (gate / (1.0 + jnp.exp(-gate)) * up).astype(jnp.bfloat16).astype(jnp.float32)
        extra = rows_ref[:, depth:].astype(jnp.float32)
        coefficient = jnp.sum(extra * own, axis=1, keepdims=True)
        scaled_ref[...] = (hidden * coefficient).astype(jnp.bfloat16)
        picked = jnp.dot(pick_ref[...], scaled_ref[...], preferred_element_type=jnp.float32)
        picked = picked.astype(jnp.bfloat16)
        send_ref[:half, :] = picked[:half]
        keep_ref[:half, :] = picked[half:]
        slab_copy.wait()

    return pl.pallas_call(
        kernel,
        out_shape=(jax.ShapeDtypeStruct((half + depth, 128), jnp.bfloat16),) * 2
        + (jax.ShapeDtypeStruct(weights.shape, jnp.bfloat16),),
        in_specs=[
            pl.BlockSpec(memory_space=pltpu.SMEM),
            pl.BlockSpec(memory_space=pltpu.VMEM),
            pl.BlockSpec(memory_space=pltpu.HBM),
            pl.BlockSpec(memory_space=pltpu.VMEM),
        ],
        out_specs=(pl.BlockSpec(memory_space=pltpu.VMEM),) * 2 + (pl.BlockSpec(memory_space=pltpu.HBM),),
        scratch_shapes=[
            pltpu.VMEM(rows_ext.shape, jnp.bfloat16),
            pltpu.VMEM((row_count, 128), jnp.bfloat16),
            pltpu.SemaphoreType.DMA((2,)),
        ],
        compiler_params=pltpu.CompilerParams(vmem_limit_bytes=50 * 2**20),
    )(expert_id, pick, rows_ext, weights)


def pair_outputs(kept, received):
    chips = YS * ZHS * XS
    half = chips * 4
    depth = kept.shape[0] - half
    lanes = depth // 128

    def kernel(kept_ref, recv_ref, out_ref, part_ref):
        for k in range(4):
            span = slice(half + k * depth // 4, half + (k + 1) * depth // 4)
            part_ref[:, k * depth // 4 : (k + 1) * depth // 4] = sum(
                lax.dot_general(
                    ref[:half, :], ref[span, :], (((1,), (1,)), ((), ())), preferred_element_type=jnp.float32
                )
                for ref in (kept_ref, recv_ref)
            )
        low = lax.broadcasted_iota(jnp.int32, (chips // 2, 8, 128), 1) < 4

        def tile(q):
            return part_ref[:, q * 128 : (q + 1) * 128].reshape(chips // 2, 8, 128)

        for q in range(0, lanes, 4):
            first, second = [], []
            for p in (q, q + 2):
                a, b = tile(p), tile(p + 1)
                first.append(jnp.where(low, a, pltpu.roll(b, 4, 1)))
                second.append(jnp.where(low, pltpu.roll(a, 4, 1), b))
            out_ref[:, 0, 4 * q : 4 * q + 16, :] = jnp.concatenate(first, axis=1).astype(jnp.bfloat16)
            out_ref[:, 1, 4 * q : 4 * q + 16, :] = jnp.concatenate(second, axis=1).astype(jnp.bfloat16)

    out = pl.pallas_call(
        kernel,
        out_shape=jax.ShapeDtypeStruct((chips // 2, 2, 4 * lanes, 128), jnp.bfloat16),
        in_specs=[pl.BlockSpec(memory_space=pltpu.VMEM)] * 2,
        out_specs=pl.BlockSpec(memory_space=pltpu.VMEM),
        scratch_shapes=[pltpu.VMEM((half, depth), jnp.float32)],
        compiler_params=pltpu.CompilerParams(vmem_limit_bytes=24 * 2**20),
    )(kept, received)
    return out.reshape(chips, 4 * lanes, 128)


def sum_chunks(chunks):
    count, tall, _ = chunks.shape
    lanes = tall // 4

    def kernel(ref, out_ref):
        total = ref[0].astype(jnp.float32)
        for k in range(1, count):
            total += ref[k].astype(jnp.float32)
        out_ref[...] = jnp.concatenate(
            [total[4 * q : 4 * q + 4, :] for q in range(lanes)], axis=1
        ).astype(jnp.bfloat16)

    return pl.pallas_call(
        kernel,
        out_shape=jax.ShapeDtypeStruct((4, lanes * 128), jnp.bfloat16),
        in_specs=[pl.BlockSpec(memory_space=pltpu.VMEM)],
        out_specs=pl.BlockSpec(memory_space=pltpu.VMEM),
        compiler_params=pltpu.CompilerParams(vmem_limit_bytes=32 * 2**20),
    )(chunks)


def per_device(
    master_weights,
    first_moment,
    second_moment,
    gradient,
    placement,
    tokens,
    routed_expert_index,
    gate_weights,
):
    group = lax.axis_index("g")
    core = lax.axis_index("c")
    place = lax.axis_index(ALONG)
    row_count, depth = tokens.shape[1:]
    width = depth + EXTRA

    experts = jnp.arange(EXPERT_COUNT, dtype=jnp.int32)
    named = routed_expert_index[0][:, :, None] == experts[None, None, :]
    coefficient = jnp.sum(jnp.where(named, gate_weights[0][:, :, None], 0.0), axis=1)
    high = coefficient.astype(jnp.bfloat16)
    low = (coefficient - high.astype(jnp.float32)).astype(jnp.bfloat16)
    fill = jnp.zeros((row_count, EXTRA - 2 * EXPERT_COUNT), jnp.bfloat16)
    own_rows = jnp.concatenate([tokens[0], high, low, fill], axis=1)
    other_rows = lax.ppermute(own_rows, "zh", [(0, 1), (1, 0)])
    grad_float = gradient.astype(jnp.float32)
    first_new = beta_one * first_moment + (1.0 - beta_one) * grad_float
    second_new = beta_two * second_moment + (1.0 - beta_two) * grad_float * grad_float
    update = (
        first_new
        / (1.0 - beta_one**adam_step)
        / (jnp.sqrt(second_new / (1.0 - beta_two**adam_step)) + adam_eps)
    )
    master_out = master_weights - learn_rate * (update + weight_decay * master_weights)
    rounded = master_out.astype(jnp.bfloat16)

    other_rows, _ = lax.optimization_barrier((other_rows, rounded))
    first = lax.axis_index("zh") == 0
    pair = jnp.concatenate(
        [jnp.where(first, own_rows, other_rows), jnp.where(first, other_rows, own_rows)], axis=0
    )
    column = lax.all_gather(jnp.pad(pair, ((0, ROOM - ZHS * row_count), (0, 0))), "y", axis=0, tiled=True)

    parts = [rounded] + [
        lax.ppermute(rounded, "g", [(i, (i + s) % GROUPS) for i in range(GROUPS)])
        for s in range(1, GROUPS)
    ]
    parts, column = lax.optimization_barrier((parts, column))

    column = column.reshape(YS, ROOM, width)[:, : ZHS * row_count].reshape(-1, width)
    all_rows = lax.all_gather(column, ("x", "c"), axis=0, tiled=True)

    unit_count = placement.shape[1]
    unit_ids = jnp.arange(unit_count, dtype=jnp.int32)
    own_row = lax.dynamic_index_in_dim(placement, group, 0, keepdims=False)
    by_group = own_row.reshape(GROUPS, -1)
    places = jnp.take(by_group, (group - jnp.arange(GROUPS)) % GROUPS, axis=0).reshape(-1)
    ordered = place_slabs(places, parts)
    own_slab = lax.all_to_all(ordered, ALONG, split_axis=0, concat_axis=0, tiled=True)
    weights = own_slab.reshape(depth, -1)

    by_place = jnp.arange(all_rows.shape[0], dtype=jnp.int32).reshape(XS, CORES, YS * ZHS, row_count)
    by_place = by_place.transpose(1, 2, 0, 3).reshape(CORES, -1)
    source = jnp.where(core == 0, by_place[::-1], by_place).reshape(-1)
    pick = (source[:, None] == jnp.arange(all_rows.shape[0], dtype=jnp.int32)[None, :]).astype(jnp.bfloat16)

    slabs_each = unit_count // EXPERT_COUNT
    expert_id = jnp.sum(jnp.where(own_row == place, unit_ids, 0), keepdims=True) // slabs_each
    sent, kept, slab = hidden_units(expert_id, pick, all_rows, weights)
    received = lax.ppermute(sent, "c", [(0, 1), (1, 0)])
    chunks = pair_outputs(kept, received)
    chunks = lax.all_to_all(chunks, ("y", "zh", "x"), split_axis=0, concat_axis=0, tiled=True)
    decoded = sum_chunks(chunks)
    return (master_out, slab[None, None], decoded[None])


def solution(mesh):
    names = ("g",) + ALONG
    fine = Mesh(mesh.devices.reshape(GROUPS, YS, ZHS, XS, CORES), names)
    split = P("g", ALONG, None)
    return jax.shard_map(
        per_device,
        mesh=fine,
        in_specs=(split, split, split, split, P(), split, split, split),
        out_specs=(split, P("g", ALONG, None, None), split),
        check_vma=False,
    )
```

```python
import jax
import jax.numpy as jnp
from jax import lax
from jax.experimental import pallas as pl
from jax.experimental.pallas import tpu as pltpu
from jax.sharding import Mesh, PartitionSpec as P

adam_step = 1000.0
adam_eps = 1e-08
learn_rate = 0.005
weight_decay = 0.1
beta_one = 0.9
beta_two = 0.999

GROUPS, YS, ZHS, XS, CORES = 4, 8, 2, 4, 2
ALONG = ("y", "zh", "x", "c")
EXPERT_COUNT = 16
EXTRA = 128


def extend_rows(tokens, routed, gates):
    _, row_count, depth = tokens.shape
    top = routed.shape[2]

    def kernel(tokens_ref, routed_ref, gates_ref, out_ref):
        lane = lax.broadcasted_iota(jnp.int32, (row_count, EXTRA), 1)
        expert = jnp.where(lane < EXPERT_COUNT, lane, lane - EXPERT_COUNT)
        routed_here, gates_here = routed_ref[0], gates_ref[0]
        coefficient = jnp.zeros((row_count, EXTRA), jnp.float32)
        for k in range(top):
            named = routed_here[:, k : k + 1] == expert
            coefficient += jnp.where(named, gates_here[:, k : k + 1], 0.0)
        high = coefficient.astype(jnp.bfloat16).astype(jnp.float32)
        extra = jnp.where(lane < EXPERT_COUNT, high, coefficient - high)
        out_ref[:, :depth] = tokens_ref[0]
        out_ref[:, depth:] = jnp.where(lane < 2 * EXPERT_COUNT, extra, 0.0).astype(jnp.bfloat16)

    return pl.pallas_call(
        kernel,
        out_shape=jax.ShapeDtypeStruct((row_count, depth + EXTRA), jnp.bfloat16),
        in_specs=[pl.BlockSpec(memory_space=pltpu.VMEM)] * 3,
        out_specs=pl.BlockSpec(memory_space=pltpu.VMEM),
    )(tokens, routed, gates)


def place_slabs(group, placement, parts):
    count, rows, cols = parts[0].shape
    total = count * len(parts)

    def kernel(group_ref, placement_ref, a, b, c, d, out_ref):
        own = group_ref[0]
        for k, ref in enumerate((a, b, c, d)):
            base = ((own + len(parts) - k) % len(parts)) * count

            def body(i, _, ref=ref, base=base):
                out_ref[placement_ref[own, base + i]] = ref[i]
                return 0

            lax.fori_loop(0, count, body, 0, unroll=8)

    return pl.pallas_call(
        kernel,
        out_shape=jax.ShapeDtypeStruct((total, rows, cols), parts[0].dtype),
        in_specs=[pl.BlockSpec(memory_space=pltpu.SMEM)] * 2 + [pl.BlockSpec(memory_space=pltpu.VMEM)] * 4,
        out_specs=pl.BlockSpec(memory_space=pltpu.VMEM),
        compiler_params=pltpu.CompilerParams(vmem_limit_bytes=16 * 2**20),
    )(group, placement, *parts)


def hidden_units(expert_id, pick, rows_ext, weights):
    row_count = rows_ext.shape[0]
    depth = weights.shape[0]
    half = row_count // CORES
    blocks = 8
    block, piece = row_count // blocks, depth // blocks

    def kernel(expert_ref, pick_ref, rows_hbm, w_ref, send_ref, keep_ref, slab_hbm, rows_ref, scaled_ref, sems):
        rows_copies = [
            pltpu.make_async_copy(
                rows_hbm.at[pl.ds(k * block, block)], rows_ref.at[pl.ds(k * block, block)], sems.at[k]
            )
            for k in range(blocks)
        ]
        slab_copies = [
            pltpu.make_async_copy(
                w_ref.at[pl.ds(k * piece, piece)], slab_hbm.at[pl.ds(k * piece, piece)], sems.at[blocks + k]
            )
            for k in range(blocks)
        ]
        for copy in rows_copies + slab_copies:
            copy.start()
        send_ref[half:, :] = w_ref[:, 256:]
        keep_ref[half:, :] = w_ref[:, 256:]
        expert = expert_ref[0]
        lane = lax.broadcasted_iota(jnp.int32, (1, EXTRA), 1)
        own = jnp.where((lane == expert) | (lane == expert + EXPERT_COUNT), 1.0, 0.0)
        for copy in rows_copies:
            copy.wait()
        gate_up = jnp.dot(
            rows_ref[:, :depth], w_ref[:, :256], preferred_element_type=jnp.float32
        )
        gate, up = gate_up[:, :128], gate_up[:, 128:]
        hidden = (gate / (1.0 + jnp.exp(-gate)) * up).astype(jnp.bfloat16).astype(jnp.float32)
        extra = rows_ref[:, depth:].astype(jnp.float32)
        coefficient = jnp.sum(extra * own, axis=1, keepdims=True)
        scaled_ref[...] = (hidden * coefficient).astype(jnp.bfloat16)
        picked = jnp.dot(pick_ref[...], scaled_ref[...], preferred_element_type=jnp.float32)
        picked = picked.astype(jnp.bfloat16)
        send_ref[:half, :] = picked[:half]
        keep_ref[:half, :] = picked[half:]
        for copy in slab_copies:
            copy.wait()

    return pl.pallas_call(
        kernel,
        out_shape=(jax.ShapeDtypeStruct((half + depth, 128), jnp.bfloat16),) * 2
        + (jax.ShapeDtypeStruct(weights.shape, jnp.bfloat16),),
        in_specs=[
            pl.BlockSpec(memory_space=pltpu.SMEM),
            pl.BlockSpec(memory_space=pltpu.VMEM),
            pl.BlockSpec(memory_space=pltpu.HBM),
            pl.BlockSpec(memory_space=pltpu.VMEM),
        ],
        out_specs=(pl.BlockSpec(memory_space=pltpu.VMEM),) * 2 + (pl.BlockSpec(memory_space=pltpu.HBM),),
        scratch_shapes=[
            pltpu.VMEM(rows_ext.shape, jnp.bfloat16),
            pltpu.VMEM((row_count, 128), jnp.bfloat16),
            pltpu.SemaphoreType.DMA((2 * blocks,)),
        ],
        compiler_params=pltpu.CompilerParams(vmem_limit_bytes=50 * 2**20),
    )(expert_id, pick, rows_ext, weights)


def pair_outputs(kept, received):
    chips = YS * ZHS * XS
    half = chips * 4
    depth = kept.shape[0] - half
    lanes = depth // 128

    def kernel(kept_ref, recv_ref, out_ref, part_ref):
        for k in range(4):
            span = slice(half + k * depth // 4, half + (k + 1) * depth // 4)
            part_ref[:, k * depth // 4 : (k + 1) * depth // 4] = sum(
                lax.dot_general(
                    ref[:half, :], ref[span, :], (((1,), (1,)), ((), ())), preferred_element_type=jnp.float32
                )
                for ref in (kept_ref, recv_ref)
            )
        low = lax.broadcasted_iota(jnp.int32, (chips // 2, 8, 128), 1) < 4

        def tile(q):
            return part_ref[:, q * 128 : (q + 1) * 128].reshape(chips // 2, 8, 128)

        for q in range(0, lanes, 4):
            first, second = [], []
            for p in (q, q + 2):
                a, b = tile(p), tile(p + 1)
                first.append(jnp.where(low, a, pltpu.roll(b, 4, 1)))
                second.append(jnp.where(low, pltpu.roll(a, 4, 1), b))
            out_ref[:, 0, 4 * q : 4 * q + 16, :] = jnp.concatenate(first, axis=1).astype(jnp.bfloat16)
            out_ref[:, 1, 4 * q : 4 * q + 16, :] = jnp.concatenate(second, axis=1).astype(jnp.bfloat16)

    out = pl.pallas_call(
        kernel,
        out_shape=jax.ShapeDtypeStruct((chips // 2, 2, 4 * lanes, 128), jnp.bfloat16),
        in_specs=[pl.BlockSpec(memory_space=pltpu.VMEM)] * 2,
        out_specs=pl.BlockSpec(memory_space=pltpu.VMEM),
        scratch_shapes=[pltpu.VMEM((half, depth), jnp.float32)],
        compiler_params=pltpu.CompilerParams(vmem_limit_bytes=24 * 2**20),
    )(kept, received)
    return out.reshape(chips, 4 * lanes, 128)


def sum_chunks(chunks):
    count, tall, _ = chunks.shape
    lanes = tall // 4

    def kernel(ref, out_ref):
        total = ref[0].astype(jnp.float32)
        for k in range(1, count):
            total += ref[k].astype(jnp.float32)
        out_ref[...] = jnp.concatenate(
            [total[4 * q : 4 * q + 4, :] for q in range(lanes)], axis=1
        ).astype(jnp.bfloat16)

    return pl.pallas_call(
        kernel,
        out_shape=jax.ShapeDtypeStruct((4, lanes * 128), jnp.bfloat16),
        in_specs=[pl.BlockSpec(memory_space=pltpu.VMEM)],
        out_specs=pl.BlockSpec(memory_space=pltpu.VMEM),
        compiler_params=pltpu.CompilerParams(vmem_limit_bytes=32 * 2**20),
    )(chunks)


def per_device(
    master_weights,
    first_moment,
    second_moment,
    gradient,
    placement,
    tokens,
    routed_expert_index,
    gate_weights,
):
    group = lax.axis_index("g")
    core = lax.axis_index("c")
    place = lax.axis_index(ALONG)
    row_count, depth = tokens.shape[1:]

    own_rows = extend_rows(tokens, routed_expert_index, gate_weights)
    other_rows = lax.ppermute(own_rows, "zh", [(0, 1), (1, 0)])

    grad_float = gradient.astype(jnp.float32)
    first_new = beta_one * first_moment + (1.0 - beta_one) * grad_float
    second_new = beta_two * second_moment + (1.0 - beta_two) * grad_float * grad_float
    update = (
        first_new
        / (1.0 - beta_one**adam_step)
        / (jnp.sqrt(second_new / (1.0 - beta_two**adam_step)) + adam_eps)
    )
    master_out = master_weights - learn_rate * (update + weight_decay * master_weights)
    rounded = master_out.astype(jnp.bfloat16)

    other_rows, _ = lax.optimization_barrier((other_rows, rounded))
    pair = jnp.concatenate([own_rows, other_rows], axis=0)
    column = lax.all_gather(pair, "y", axis=0, tiled=True)

    parts = [rounded] + [
        lax.ppermute(rounded, "g", [(i, (i + s) % GROUPS) for i in range(GROUPS)])
        for s in range(1, GROUPS)
    ]
    parts, column = lax.optimization_barrier((parts, column))

    all_rows = lax.all_gather(column, ("x", "c"), axis=0, tiled=True)

    unit_count = placement.shape[1]
    unit_ids = jnp.arange(unit_count, dtype=jnp.int32)
    own_row = lax.dynamic_index_in_dim(placement, group, 0, keepdims=False)
    ordered = place_slabs(jnp.full((1,), group, jnp.int32), placement, parts)
    own_slab = lax.all_to_all(ordered, ALONG, split_axis=0, concat_axis=0, tiled=True)
    weights = own_slab.reshape(depth, -1)

    row_ids = jnp.arange(all_rows.shape[0], dtype=jnp.int32)
    half = all_rows.shape[0] // CORES
    i, x, y_zh = row_ids % row_count, row_ids // row_count % XS, row_ids % half // (row_count * XS)
    of_core = jnp.where(row_ids < half, 1 - core, core)
    here = lax.axis_index("zh")
    source = ((x * CORES + of_core) * (YS * ZHS) + (y_zh ^ here)) * row_count + i
    pick = (source[:, None] == row_ids[None, :]).astype(jnp.bfloat16)

    slabs_each = unit_count // EXPERT_COUNT
    expert_id = jnp.sum(jnp.where(own_row == place, unit_ids, 0), keepdims=True) // slabs_each
    sent, kept, slab = hidden_units(expert_id, pick, all_rows, weights)
    received = lax.ppermute(sent, "c", [(0, 1), (1, 0)])
    chunks = pair_outputs(kept, received)
    chunks = lax.all_to_all(chunks, ("y", "zh", "x"), split_axis=0, concat_axis=0, tiled=True)
    decoded = sum_chunks(chunks)
    return (master_out, slab[None, None], decoded[None])


def solution(mesh):
    names = ("g",) + ALONG
    fine = Mesh(mesh.devices.reshape(GROUPS, YS, ZHS, XS, CORES), names)
    split = P("g", ALONG, None)
    return jax.shard_map(
        per_device,
        mesh=fine,
        in_specs=(split, split, split, split, P(), split, split, split),
        out_specs=(split, P("g", ALONG, None, None), split),
        check_vma=False,
    )
```

```python
import jax
import jax.numpy as jnp
from jax import lax
from jax.experimental import pallas as pl
from jax.experimental.pallas import tpu as pltpu
from jax.sharding import Mesh, PartitionSpec as P

adam_step = 1000.0
adam_eps = 1e-08
learn_rate = 0.005
weight_decay = 0.1
beta_one = 0.9
beta_two = 0.999

GROUPS, YS, ZHS, XS, CORES = 4, 8, 2, 4, 2
ALONG = ("y", "zh", "x", "c")
EXPERT_COUNT = 16
EXTRA = 128


def extend_rows(copies, tokens, routed, gates):
    _, row_count, depth = tokens.shape
    top = routed.shape[2]

    def kernel(tokens_ref, routed_ref, gates_ref, out_ref):
        lane = lax.broadcasted_iota(jnp.int32, (row_count, EXTRA), 1)
        expert = jnp.where(lane < EXPERT_COUNT, lane, lane - EXPERT_COUNT)
        routed_here, gates_here = routed_ref[0], gates_ref[0]
        coefficient = jnp.zeros((row_count, EXTRA), jnp.float32)
        for k in range(top):
            named = routed_here[:, k : k + 1] == expert
            coefficient += jnp.where(named, gates_here[:, k : k + 1], 0.0)
        high = coefficient.astype(jnp.bfloat16).astype(jnp.float32)
        extra = jnp.where(lane < EXPERT_COUNT, high, coefficient - high)
        extra = jnp.where(lane < 2 * EXPERT_COUNT, extra, 0.0).astype(jnp.bfloat16)
        for k in range(copies):
            out_ref[k, :, :depth] = tokens_ref[0]
            out_ref[k, :, depth:] = extra

    return pl.pallas_call(
        kernel,
        out_shape=jax.ShapeDtypeStruct((copies, row_count, depth + EXTRA), jnp.bfloat16),
        in_specs=[pl.BlockSpec(memory_space=pltpu.VMEM)] * 3,
        out_specs=pl.BlockSpec(memory_space=pltpu.VMEM),
    )(tokens, routed, gates)


def place_slabs(group, placement, parts):
    count, rows, cols = parts[0].shape
    total = count * len(parts)

    def kernel(group_ref, placement_ref, a, b, c, d, out_ref):
        own = group_ref[0]
        for k, ref in enumerate((a, b, c, d)):
            base = ((own + len(parts) - k) % len(parts)) * count

            def body(i, _, ref=ref, base=base):
                out_ref[placement_ref[own, base + i]] = ref[i]
                return 0

            lax.fori_loop(0, count, body, 0, unroll=8)

    return pl.pallas_call(
        kernel,
        out_shape=jax.ShapeDtypeStruct((total, rows, cols), parts[0].dtype),
        in_specs=[pl.BlockSpec(memory_space=pltpu.SMEM)] * 2 + [pl.BlockSpec(memory_space=pltpu.VMEM)] * 4,
        out_specs=pl.BlockSpec(memory_space=pltpu.VMEM),
        compiler_params=pltpu.CompilerParams(vmem_limit_bytes=16 * 2**20),
    )(group, placement, *parts)


def hidden_units(expert_id, pick, own_rows, other_rows, weights):
    half = own_rows.shape[0]
    depth = weights.shape[0]
    blocks = 4
    piece = depth // blocks

    def kernel(expert_ref, pick_ref, own_ref, other_ref, w_ref, send_ref, keep_ref, slab_hbm, sems):
        slab_copies = [
            pltpu.make_async_copy(
                w_ref.at[pl.ds(k * piece, piece)], slab_hbm.at[pl.ds(k * piece, piece)], sems.at[k]
            )
            for k in range(blocks)
        ]
        for copy in slab_copies:
            copy.start()
        expert = expert_ref[0]
        lane = lax.broadcasted_iota(jnp.int32, (1, EXTRA), 1)
        own = jnp.where((lane == expert) | (lane == expert + EXPERT_COUNT), 1.0, 0.0)
        for rows_ref, out_ref in ((other_ref, send_ref), (own_ref, keep_ref)):
            gate_up = jnp.dot(rows_ref[:, :depth], w_ref[:, :256], preferred_element_type=jnp.float32)
            gate, up = gate_up[:, :128], gate_up[:, 128:]
            hidden = (gate / (1.0 + jnp.exp(-gate)) * up).astype(jnp.bfloat16).astype(jnp.float32)
            extra = rows_ref[:, depth:].astype(jnp.float32)
            coefficient = jnp.sum(extra * own, axis=1, keepdims=True)
            scaled = (hidden * coefficient).astype(jnp.bfloat16)
            ordered = jnp.dot(pick_ref[...], scaled, preferred_element_type=jnp.float32)
            out_ref[:half, :] = ordered.astype(jnp.bfloat16)
            out_ref[half:, :] = w_ref[:, 256:]
        for copy in slab_copies:
            copy.wait()

    return pl.pallas_call(
        kernel,
        out_shape=(jax.ShapeDtypeStruct((half + depth, 128), jnp.bfloat16),) * 2
        + (jax.ShapeDtypeStruct(weights.shape, jnp.bfloat16),),
        in_specs=[pl.BlockSpec(memory_space=pltpu.SMEM)] + [pl.BlockSpec(memory_space=pltpu.VMEM)] * 4,
        out_specs=(pl.BlockSpec(memory_space=pltpu.VMEM),) * 2 + (pl.BlockSpec(memory_space=pltpu.HBM),),
        scratch_shapes=[pltpu.SemaphoreType.DMA((blocks,))],
        compiler_params=pltpu.CompilerParams(vmem_limit_bytes=24 * 2**20),
    )(expert_id, pick, own_rows, other_rows, weights)


def pair_outputs(kept, received):
    chips = YS * ZHS * XS
    half = chips * 4
    depth = kept.shape[0] - half
    lanes = depth // 128

    def kernel(kept_ref, recv_ref, out_ref, part_ref):
        for k in range(4):
            span = slice(half + k * depth // 4, half + (k + 1) * depth // 4)
            part_ref[:, k * depth // 4 : (k + 1) * depth // 4] = sum(
                lax.dot_general(
                    ref[:half, :], ref[span, :], (((1,), (1,)), ((), ())), preferred_element_type=jnp.float32
                )
                for ref in (kept_ref, recv_ref)
            )
        low = lax.broadcasted_iota(jnp.int32, (chips // 2, 8, 128), 1) < 4

        def tile(q):
            return part_ref[:, q * 128 : (q + 1) * 128].reshape(chips // 2, 8, 128)

        for q in range(0, lanes, 4):
            first, second = [], []
            for p in (q, q + 2):
                a, b = tile(p), tile(p + 1)
                first.append(jnp.where(low, a, pltpu.roll(b, 4, 1)))
                second.append(jnp.where(low, pltpu.roll(a, 4, 1), b))
            out_ref[:, 0, 4 * q : 4 * q + 16, :] = jnp.concatenate(first, axis=1).astype(jnp.bfloat16)
            out_ref[:, 1, 4 * q : 4 * q + 16, :] = jnp.concatenate(second, axis=1).astype(jnp.bfloat16)

    out = pl.pallas_call(
        kernel,
        out_shape=jax.ShapeDtypeStruct((chips // 2, 2, 4 * lanes, 128), jnp.bfloat16),
        in_specs=[pl.BlockSpec(memory_space=pltpu.VMEM)] * 2,
        out_specs=pl.BlockSpec(memory_space=pltpu.VMEM),
        scratch_shapes=[pltpu.VMEM((half, depth), jnp.float32)],
        compiler_params=pltpu.CompilerParams(vmem_limit_bytes=24 * 2**20),
    )(kept, received)
    return out.reshape(chips, 4 * lanes, 128)


def sum_chunks(chunks):
    count, tall, _ = chunks.shape
    lanes = tall // 4

    def kernel(ref, out_ref):
        total = ref[0].astype(jnp.float32)
        for k in range(1, count):
            total += ref[k].astype(jnp.float32)
        out_ref[...] = jnp.concatenate(
            [total[4 * q : 4 * q + 4, :] for q in range(lanes)], axis=1
        ).astype(jnp.bfloat16)

    return pl.pallas_call(
        kernel,
        out_shape=jax.ShapeDtypeStruct((4, lanes * 128), jnp.bfloat16),
        in_specs=[pl.BlockSpec(memory_space=pltpu.VMEM)],
        out_specs=pl.BlockSpec(memory_space=pltpu.VMEM),
        compiler_params=pltpu.CompilerParams(vmem_limit_bytes=32 * 2**20),
    )(chunks)


def per_device(
    master_weights,
    first_moment,
    second_moment,
    gradient,
    placement,
    tokens,
    routed_expert_index,
    gate_weights,
):
    group = lax.axis_index("g")
    place = lax.axis_index(ALONG)
    row_count, depth = tokens.shape[1:]

    own_rows = extend_rows(1, tokens, routed_expert_index, gate_weights)[0]
    other_rows = lax.ppermute(own_rows, "zh", [(0, 1), (1, 0)])

    grad_float = gradient.astype(jnp.float32)
    first_new = beta_one * first_moment + (1.0 - beta_one) * grad_float
    second_new = beta_two * second_moment + (1.0 - beta_two) * grad_float * grad_float
    update = (
        first_new
        / (1.0 - beta_one**adam_step)
        / (jnp.sqrt(second_new / (1.0 - beta_two**adam_step)) + adam_eps)
    )
    master_out = master_weights - learn_rate * (update + weight_decay * master_weights)
    rounded = master_out.astype(jnp.bfloat16)
    other_rows, _ = lax.optimization_barrier((other_rows, rounded))

    parts = [rounded] + [
        lax.ppermute(rounded, "g", [(i, (i + s) % GROUPS) for i in range(GROUPS)])
        for s in range(1, GROUPS)
    ]

    pair = jnp.concatenate([own_rows, other_rows], axis=0)
    column = lax.all_gather(pair, "y", axis=0, tiled=True)
    parts, column = lax.optimization_barrier((parts, column))

    others = [lax.ppermute(column, "x", [(k, (k + t) % XS) for k in range(XS)]) for t in range(1, XS)]
    own_rows = jnp.concatenate([column] + others, axis=0)
    other_rows = lax.ppermute(own_rows, "c", [(0, 1), (1, 0)])

    unit_count = placement.shape[1]
    unit_ids = jnp.arange(unit_count, dtype=jnp.int32)
    own_row = lax.dynamic_index_in_dim(placement, group, 0, keepdims=False)
    ordered = place_slabs(jnp.full((1,), group, jnp.int32), placement, parts)
    own_slab = lax.all_to_all(ordered, ALONG, split_axis=0, concat_axis=0, tiled=True)
    weights = own_slab.reshape(depth, -1)

    row_ids = jnp.arange(own_rows.shape[0], dtype=jnp.int32)
    i, x, y_zh = row_ids % row_count, row_ids // row_count % XS, row_ids // (row_count * XS)
    away = (lax.axis_index("x") + XS - x) % XS
    source = (away * (YS * ZHS) + (y_zh ^ lax.axis_index("zh"))) * row_count + i
    pick = (source[:, None] == row_ids[None, :]).astype(jnp.bfloat16)

    slabs_each = unit_count // EXPERT_COUNT
    expert_id = jnp.sum(jnp.where(own_row == place, unit_ids, 0), keepdims=True) // slabs_each
    sent, kept, slab = hidden_units(expert_id, pick, own_rows, other_rows, weights)
    received = lax.ppermute(sent, "c", [(0, 1), (1, 0)])
    chunks = pair_outputs(kept, received)
    chunks = lax.all_to_all(chunks, ("y", "zh", "x"), split_axis=0, concat_axis=0, tiled=True)
    decoded = sum_chunks(chunks)
    return (master_out, slab[None, None], decoded[None])


def solution(mesh):
    names = ("g",) + ALONG
    fine = Mesh(mesh.devices.reshape(GROUPS, YS, ZHS, XS, CORES), names)
    split = P("g", ALONG, None)
    return jax.shard_map(
        per_device,
        mesh=fine,
        in_specs=(split, split, split, split, P(), split, split, split),
        out_specs=(split, P("g", ALONG, None, None), split),
        check_vma=False,
    )
```

```python
import jax
import jax.numpy as jnp
from jax import lax
from jax.experimental import pallas as pl
from jax.experimental.pallas import tpu as pltpu
from jax.sharding import Mesh, PartitionSpec as P

adam_step = 1000.0
adam_eps = 1e-08
learn_rate = 0.005
weight_decay = 0.1
beta_one = 0.9
beta_two = 0.999

GROUPS, YS, ZHS, XS, CORES = 4, 8, 2, 4, 2
ALONG = ("y", "zh", "x", "c")
EXPERT_COUNT = 16
EXTRA = 128


def extend_rows(copies, tokens, routed, gates):
    _, row_count, depth = tokens.shape
    top = routed.shape[2]

    def kernel(tokens_ref, routed_ref, gates_ref, out_ref):
        lane = lax.broadcasted_iota(jnp.int32, (row_count, EXTRA), 1)
        expert = jnp.where(lane < EXPERT_COUNT, lane, lane - EXPERT_COUNT)
        routed_here, gates_here = routed_ref[0], gates_ref[0]
        coefficient = jnp.zeros((row_count, EXTRA), jnp.float32)
        for k in range(top):
            named = routed_here[:, k : k + 1] == expert
            coefficient += jnp.where(named, gates_here[:, k : k + 1], 0.0)
        high = coefficient.astype(jnp.bfloat16).astype(jnp.float32)
        extra = jnp.where(lane < EXPERT_COUNT, high, coefficient - high)
        extra = jnp.where(lane < 2 * EXPERT_COUNT, extra, 0.0).astype(jnp.bfloat16)
        for k in range(copies):
            out_ref[k, :, :depth] = tokens_ref[0]
            out_ref[k, :, depth:] = extra

    return pl.pallas_call(
        kernel,
        out_shape=jax.ShapeDtypeStruct((copies, row_count, depth + EXTRA), jnp.bfloat16),
        in_specs=[pl.BlockSpec(memory_space=pltpu.VMEM)] * 3,
        out_specs=pl.BlockSpec(memory_space=pltpu.VMEM),
    )(tokens, routed, gates)


def place_slabs(group, placement, parts):
    count, rows, cols = parts[0].shape
    total = count * len(parts)

    def kernel(group_ref, placement_ref, a, b, c, d, out_ref):
        own = group_ref[0]
        for k, ref in enumerate((a, b, c, d)):
            base = ((own + k) % len(parts)) * count

            def body(i, _, ref=ref, base=base):
                out_ref[placement_ref[own, base + i]] = ref[i]
                return 0

            lax.fori_loop(0, count, body, 0, unroll=8)

    return pl.pallas_call(
        kernel,
        out_shape=jax.ShapeDtypeStruct((total, rows, cols), parts[0].dtype),
        in_specs=[pl.BlockSpec(memory_space=pltpu.SMEM)] * 2 + [pl.BlockSpec(memory_space=pltpu.VMEM)] * 4,
        out_specs=pl.BlockSpec(memory_space=pltpu.VMEM),
        compiler_params=pltpu.CompilerParams(vmem_limit_bytes=16 * 2**20),
    )(group, placement, *parts)


def hidden_units(expert_id, pick, rows, weights, with_slab):
    half = rows.shape[0]
    depth = weights.shape[0]
    blocks = 4
    piece = depth // blocks

    def kernel(expert_ref, pick_ref, rows_ref, w_ref, out_ref, *slab):
        copies = []
        if with_slab:
            slab_hbm, sems = slab
            copies = [
                pltpu.make_async_copy(
                    w_ref.at[pl.ds(k * piece, piece)], slab_hbm.at[pl.ds(k * piece, piece)], sems.at[k]
                )
                for k in range(blocks)
            ]
        for copy in copies:
            copy.start()
        out_ref[half:, :] = w_ref[:, 256:]
        expert = expert_ref[0]
        lane = lax.broadcasted_iota(jnp.int32, (1, EXTRA), 1)
        own = jnp.where((lane == expert) | (lane == expert + EXPERT_COUNT), 1.0, 0.0)
        gate_up = jnp.dot(rows_ref[:, :depth], w_ref[:, :256], preferred_element_type=jnp.float32)
        gate, up = gate_up[:, :128], gate_up[:, 128:]
        hidden = (gate / (1.0 + jnp.exp(-gate)) * up).astype(jnp.bfloat16).astype(jnp.float32)
        extra = rows_ref[:, depth:].astype(jnp.float32)
        coefficient = jnp.sum(extra * own, axis=1, keepdims=True)
        scaled = (hidden * coefficient).astype(jnp.bfloat16)
        ordered = jnp.dot(pick_ref[...], scaled, preferred_element_type=jnp.float32)
        out_ref[:half, :] = ordered.astype(jnp.bfloat16)
        for copy in copies:
            copy.wait()

    out_shape = (jax.ShapeDtypeStruct((half + depth, 128), jnp.bfloat16),)
    out_specs = (pl.BlockSpec(memory_space=pltpu.VMEM),)
    if with_slab:
        out_shape += (jax.ShapeDtypeStruct(weights.shape, jnp.bfloat16),)
        out_specs += (pl.BlockSpec(memory_space=pltpu.HBM),)
    return pl.pallas_call(
        kernel,
        out_shape=out_shape,
        in_specs=[pl.BlockSpec(memory_space=pltpu.SMEM)] + [pl.BlockSpec(memory_space=pltpu.VMEM)] * 3,
        out_specs=out_specs,
        scratch_shapes=[pltpu.SemaphoreType.DMA((blocks,))] if with_slab else [],
        compiler_params=pltpu.CompilerParams(vmem_limit_bytes=24 * 2**20),
    )(expert_id, pick, rows, weights)


def pair_outputs(kept, received):
    chips = YS * ZHS * XS
    half = chips * 4
    depth = kept.shape[0] - half
    lanes = depth // 128

    def kernel(kept_ref, recv_ref, out_ref, part_ref):
        for k in range(4):
            span = slice(half + k * depth // 4, half + (k + 1) * depth // 4)
            part_ref[:, k * depth // 4 : (k + 1) * depth // 4] = sum(
                lax.dot_general(
                    ref[:half, :], ref[span, :], (((1,), (1,)), ((), ())), preferred_element_type=jnp.float32
                )
                for ref in (kept_ref, recv_ref)
            )
        low = lax.broadcasted_iota(jnp.int32, (chips // 2, 8, 128), 1) < 4

        def tile(q):
            return part_ref[:, q * 128 : (q + 1) * 128].reshape(chips // 2, 8, 128)

        for q in range(0, lanes, 4):
            first, second = [], []
            for p in (q, q + 2):
                a, b = tile(p), tile(p + 1)
                first.append(jnp.where(low, a, pltpu.roll(b, 4, 1)))
                second.append(jnp.where(low, pltpu.roll(a, 4, 1), b))
            out_ref[:, 0, 4 * q : 4 * q + 16, :] = jnp.concatenate(first, axis=1).astype(jnp.bfloat16)
            out_ref[:, 1, 4 * q : 4 * q + 16, :] = jnp.concatenate(second, axis=1).astype(jnp.bfloat16)

    out = pl.pallas_call(
        kernel,
        out_shape=jax.ShapeDtypeStruct((chips // 2, 2, 4 * lanes, 128), jnp.bfloat16),
        in_specs=[pl.BlockSpec(memory_space=pltpu.VMEM)] * 2,
        out_specs=pl.BlockSpec(memory_space=pltpu.VMEM),
        scratch_shapes=[pltpu.VMEM((half, depth), jnp.float32)],
        compiler_params=pltpu.CompilerParams(vmem_limit_bytes=24 * 2**20),
    )(kept, received)
    return out.reshape(chips, 4 * lanes, 128)


def sum_chunks(chunks):
    count, tall, _ = chunks.shape
    lanes = tall // 4

    def kernel(ref, out_ref):
        total = ref[0].astype(jnp.float32)
        for k in range(1, count):
            total += ref[k].astype(jnp.float32)
        out_ref[...] = jnp.concatenate(
            [total[4 * q : 4 * q + 4, :] for q in range(lanes)], axis=1
        ).astype(jnp.bfloat16)

    return pl.pallas_call(
        kernel,
        out_shape=jax.ShapeDtypeStruct((4, lanes * 128), jnp.bfloat16),
        in_specs=[pl.BlockSpec(memory_space=pltpu.VMEM)],
        out_specs=pl.BlockSpec(memory_space=pltpu.VMEM),
        compiler_params=pltpu.CompilerParams(vmem_limit_bytes=32 * 2**20),
    )(chunks)


def per_device(
    master_weights,
    first_moment,
    second_moment,
    gradient,
    placement,
    tokens,
    routed_expert_index,
    gate_weights,
):
    group = lax.axis_index("g")
    place = lax.axis_index(ALONG)
    row_count, depth = tokens.shape[1:]

    own_rows = extend_rows(1, tokens, routed_expert_index, gate_weights)[0]
    other_rows = lax.ppermute(own_rows, "zh", [(0, 1), (1, 0)])

    grad_float = gradient.astype(jnp.float32)
    first_new = beta_one * first_moment + (1.0 - beta_one) * grad_float
    second_new = beta_two * second_moment + (1.0 - beta_two) * grad_float * grad_float
    update = (
        first_new
        / (1.0 - beta_one**adam_step)
        / (jnp.sqrt(second_new / (1.0 - beta_two**adam_step)) + adam_eps)
    )
    master_out = master_weights - learn_rate * (update + weight_decay * master_weights)
    rounded = master_out.astype(jnp.bfloat16)
    other_rows, _ = lax.optimization_barrier((other_rows, rounded))

    parts = [rounded] + [
        lax.ppermute(rounded, "g", [((i + s) % GROUPS, i) for i in range(GROUPS)])
        for s in range(1, GROUPS)
    ]

    pair = jnp.concatenate([own_rows, other_rows], axis=0)
    column = lax.all_gather(pair, "y", axis=0, tiled=True)
    parts, column = lax.optimization_barrier((parts, column))

    others = [lax.ppermute(column, "x", [(k, (k + t) % XS) for k in range(XS)]) for t in range(1, XS)]
    own_rows = jnp.concatenate([column] + others, axis=0)
    other_rows = lax.ppermute(own_rows, "c", [(0, 1), (1, 0)])

    unit_count = placement.shape[1]
    unit_ids = jnp.arange(unit_count, dtype=jnp.int32)
    own_row = lax.dynamic_index_in_dim(placement, group, 0, keepdims=False)
    ordered = place_slabs(jnp.full((1,), group, jnp.int32), placement, parts)
    own_slab = lax.all_to_all(ordered, ALONG, split_axis=0, concat_axis=0, tiled=True)
    weights = own_slab.reshape(depth, -1)

    row_ids = jnp.arange(own_rows.shape[0], dtype=jnp.int32)
    i, x, y_zh = row_ids % row_count, row_ids // row_count % XS, row_ids // (row_count * XS)
    away = (lax.axis_index("x") + XS - x) % XS
    source = (away * (YS * ZHS) + (y_zh ^ lax.axis_index("zh"))) * row_count + i
    pick = (source[:, None] == row_ids[None, :]).astype(jnp.bfloat16)

    slabs_each = unit_count // EXPERT_COUNT
    expert_id = jnp.sum(jnp.where(own_row == place, unit_ids, 0), keepdims=True) // slabs_each
    kept, slab = hidden_units(expert_id, pick, own_rows, weights, True)
    (sent,) = hidden_units(expert_id, pick, other_rows, weights, False)
    received = lax.ppermute(sent, "c", [(0, 1), (1, 0)])
    chunks = pair_outputs(kept, received)
    chunks = lax.all_to_all(chunks, ("y", "zh", "x"), split_axis=0, concat_axis=0, tiled=True)
    decoded = sum_chunks(chunks)
    return (master_out, slab[None, None], decoded[None])


def solution(mesh):
    names = ("g",) + ALONG
    fine = Mesh(mesh.devices.reshape(GROUPS, YS, ZHS, XS, CORES), names)
    split = P("g", ALONG, None)
    return jax.shard_map(
        per_device,
        mesh=fine,
        in_specs=(split, split, split, split, P(), split, split, split),
        out_specs=(split, P("g", ALONG, None, None), split),
        check_vma=False,
    )
```

```python
import jax
import jax.numpy as jnp
from jax import lax
from jax.experimental import pallas as pl
from jax.experimental.pallas import tpu as pltpu
from jax.sharding import Mesh, PartitionSpec as P

adam_step = 1000.0
adam_eps = 1e-08
learn_rate = 0.005
weight_decay = 0.1
beta_one = 0.9
beta_two = 0.999

GROUPS, YS, ZHS, XS, CORES = 4, 8, 2, 4, 2
ALONG = ("y", "zh", "x", "c")
EXPERT_COUNT = 16
EXTRA = 128


def extend_rows(copies, tokens, routed, gates):
    _, row_count, depth = tokens.shape
    top = routed.shape[2]

    def kernel(tokens_ref, routed_ref, gates_ref, out_ref):
        lane = lax.broadcasted_iota(jnp.int32, (row_count, EXTRA), 1)
        expert = jnp.where(lane < EXPERT_COUNT, lane, lane - EXPERT_COUNT)
        routed_here, gates_here = routed_ref[0], gates_ref[0]
        coefficient = jnp.zeros((row_count, EXTRA), jnp.float32)
        for k in range(top):
            named = routed_here[:, k : k + 1] == expert
            coefficient += jnp.where(named, gates_here[:, k : k + 1], 0.0)
        high = coefficient.astype(jnp.bfloat16).astype(jnp.float32)
        extra = jnp.where(lane < EXPERT_COUNT, high, coefficient - high)
        extra = jnp.where(lane < 2 * EXPERT_COUNT, extra, 0.0).astype(jnp.bfloat16)
        for k in range(copies):
            out_ref[k, :, :depth] = tokens_ref[0]
            out_ref[k, :, depth:] = extra

    return pl.pallas_call(
        kernel,
        out_shape=jax.ShapeDtypeStruct((copies, row_count, depth + EXTRA), jnp.bfloat16),
        in_specs=[pl.BlockSpec(memory_space=pltpu.VMEM)] * 3,
        out_specs=pl.BlockSpec(memory_space=pltpu.VMEM),
    )(tokens, routed, gates)


def place_slabs(group, placement, parts):
    count, rows, cols = parts[0].shape
    total = count * len(parts)

    def kernel(group_ref, placement_ref, a, b, c, d, out_hbm, sem):
        own = group_ref[0]
        for k, ref in enumerate((a, b, c, d)):
            base = ((own + k) % len(parts)) * count

            def body(i, _, ref=ref, base=base):
                pltpu.make_async_copy(ref.at[i], out_hbm.at[placement_ref[own, base + i]], sem).start()
                return 0

            lax.fori_loop(0, count, body, 0, unroll=8)
        pltpu.make_async_copy(out_hbm, out_hbm, sem).wait()

    return pl.pallas_call(
        kernel,
        out_shape=jax.ShapeDtypeStruct((total, rows, cols), parts[0].dtype),
        in_specs=[pl.BlockSpec(memory_space=pltpu.SMEM)] * 2 + [pl.BlockSpec(memory_space=pltpu.VMEM)] * 4,
        out_specs=pl.BlockSpec(memory_space=pltpu.HBM),
        scratch_shapes=[pltpu.SemaphoreType.DMA],
        compiler_params=pltpu.CompilerParams(vmem_limit_bytes=16 * 2**20),
    )(group, placement, *parts)


def hidden_units(expert_id, pick, rows, weights, with_slab):
    half = rows.shape[0]
    depth = weights.shape[0]
    blocks = 4
    piece = depth // blocks

    def kernel(expert_ref, pick_ref, rows_ref, w_ref, out_ref, *slab):
        copies = []
        if with_slab:
            slab_hbm, sems = slab
            copies = [
                pltpu.make_async_copy(
                    w_ref.at[pl.ds(k * piece, piece)], slab_hbm.at[pl.ds(k * piece, piece)], sems.at[k]
                )
                for k in range(blocks)
            ]
        for copy in copies:
            copy.start()
        out_ref[half:, :] = w_ref[:, 256:]
        expert = expert_ref[0]
        lane = lax.broadcasted_iota(jnp.int32, (1, EXTRA), 1)
        own = jnp.where((lane == expert) | (lane == expert + EXPERT_COUNT), 1.0, 0.0)
        gate_up = jnp.dot(rows_ref[:, :depth], w_ref[:, :256], preferred_element_type=jnp.float32)
        gate, up = gate_up[:, :128], gate_up[:, 128:]
        hidden = (gate / (1.0 + jnp.exp(-gate)) * up).astype(jnp.bfloat16).astype(jnp.float32)
        extra = rows_ref[:, depth:].astype(jnp.float32)
        coefficient = jnp.sum(extra * own, axis=1, keepdims=True)
        scaled = (hidden * coefficient).astype(jnp.bfloat16)
        ordered = jnp.dot(pick_ref[...], scaled, preferred_element_type=jnp.float32)
        out_ref[:half, :] = ordered.astype(jnp.bfloat16)
        for copy in copies:
            copy.wait()

    out_shape = (jax.ShapeDtypeStruct((half + depth, 128), jnp.bfloat16),)
    out_specs = (pl.BlockSpec(memory_space=pltpu.VMEM),)
    if with_slab:
        out_shape += (jax.ShapeDtypeStruct(weights.shape, jnp.bfloat16),)
        out_specs += (pl.BlockSpec(memory_space=pltpu.HBM),)
    return pl.pallas_call(
        kernel,
        out_shape=out_shape,
        in_specs=[pl.BlockSpec(memory_space=pltpu.SMEM)] + [pl.BlockSpec(memory_space=pltpu.VMEM)] * 3,
        out_specs=out_specs,
        scratch_shapes=[pltpu.SemaphoreType.DMA((blocks,))] if with_slab else [],
        compiler_params=pltpu.CompilerParams(vmem_limit_bytes=24 * 2**20),
    )(expert_id, pick, rows, weights)


def pair_outputs(kept, received):
    chips = YS * ZHS * XS
    half = chips * 4
    depth = kept.shape[0] - half
    lanes = depth // 128

    def kernel(kept_ref, recv_ref, out_ref, part_ref):
        for k in range(4):
            span = slice(half + k * depth // 4, half + (k + 1) * depth // 4)
            part_ref[:, k * depth // 4 : (k + 1) * depth // 4] = sum(
                lax.dot_general(
                    ref[:half, :], ref[span, :], (((1,), (1,)), ((), ())), preferred_element_type=jnp.float32
                )
                for ref in (kept_ref, recv_ref)
            )
        low = lax.broadcasted_iota(jnp.int32, (chips // 2, 8, 128), 1) < 4

        def tile(q):
            return part_ref[:, q * 128 : (q + 1) * 128].reshape(chips // 2, 8, 128)

        for q in range(0, lanes, 4):
            first, second = [], []
            for p in (q, q + 2):
                a, b = tile(p), tile(p + 1)
                first.append(jnp.where(low, a, pltpu.roll(b, 4, 1)))
                second.append(jnp.where(low, pltpu.roll(a, 4, 1), b))
            out_ref[:, 0, 4 * q : 4 * q + 16, :] = jnp.concatenate(first, axis=1).astype(jnp.bfloat16)
            out_ref[:, 1, 4 * q : 4 * q + 16, :] = jnp.concatenate(second, axis=1).astype(jnp.bfloat16)

    out = pl.pallas_call(
        kernel,
        out_shape=jax.ShapeDtypeStruct((chips // 2, 2, 4 * lanes, 128), jnp.bfloat16),
        in_specs=[pl.BlockSpec(memory_space=pltpu.VMEM)] * 2,
        out_specs=pl.BlockSpec(memory_space=pltpu.VMEM),
        scratch_shapes=[pltpu.VMEM((half, depth), jnp.float32)],
        compiler_params=pltpu.CompilerParams(vmem_limit_bytes=24 * 2**20),
    )(kept, received)
    return out.reshape(chips, 4 * lanes, 128)


def sum_chunks(chunks):
    count, tall, _ = chunks.shape
    lanes = tall // 4

    def kernel(ref, out_ref):
        total = ref[0].astype(jnp.float32)
        for k in range(1, count):
            total += ref[k].astype(jnp.float32)
        out_ref[...] = jnp.concatenate(
            [total[4 * q : 4 * q + 4, :] for q in range(lanes)], axis=1
        ).astype(jnp.bfloat16)

    return pl.pallas_call(
        kernel,
        out_shape=jax.ShapeDtypeStruct((4, lanes * 128), jnp.bfloat16),
        in_specs=[pl.BlockSpec(memory_space=pltpu.VMEM)],
        out_specs=pl.BlockSpec(memory_space=pltpu.VMEM),
        compiler_params=pltpu.CompilerParams(vmem_limit_bytes=32 * 2**20),
    )(chunks)


def per_device(
    master_weights,
    first_moment,
    second_moment,
    gradient,
    placement,
    tokens,
    routed_expert_index,
    gate_weights,
):
    group = lax.axis_index("g")
    place = lax.axis_index(ALONG)
    row_count, depth = tokens.shape[1:]

    own_rows = extend_rows(1, tokens, routed_expert_index, gate_weights)[0]
    other_rows = lax.ppermute(own_rows, "zh", [(0, 1), (1, 0)])

    grad_float = gradient.astype(jnp.float32)
    first_new = beta_one * first_moment + (1.0 - beta_one) * grad_float
    second_new = beta_two * second_moment + (1.0 - beta_two) * grad_float * grad_float
    update = (
        first_new
        / (1.0 - beta_one**adam_step)
        / (jnp.sqrt(second_new / (1.0 - beta_two**adam_step)) + adam_eps)
    )
    master_out = master_weights - learn_rate * (update + weight_decay * master_weights)
    rounded = master_out.astype(jnp.bfloat16)
    other_rows, _ = lax.optimization_barrier((other_rows, rounded))

    parts = [rounded] + [
        lax.ppermute(rounded, "g", [((i + s) % GROUPS, i) for i in range(GROUPS)])
        for s in range(1, GROUPS)
    ]

    pair = jnp.concatenate([own_rows, other_rows], axis=0)
    column = lax.all_gather(pair, "y", axis=0, tiled=True)
    parts, column = lax.optimization_barrier((parts, column))

    others = [lax.ppermute(column, "x", [(k, (k + t) % XS) for k in range(XS)]) for t in range(1, XS)]
    own_rows = jnp.concatenate([column] + others, axis=0)
    other_rows = lax.ppermute(own_rows, "c", [(0, 1), (1, 0)])

    unit_count = placement.shape[1]
    unit_ids = jnp.arange(unit_count, dtype=jnp.int32)
    own_row = lax.dynamic_index_in_dim(placement, group, 0, keepdims=False)
    ordered = place_slabs(jnp.full((1,), group, jnp.int32), placement, parts)
    own_slab = lax.all_to_all(ordered, ALONG, split_axis=0, concat_axis=0, tiled=True)
    weights = own_slab.reshape(depth, -1)

    row_ids = jnp.arange(own_rows.shape[0], dtype=jnp.int32)
    i, x, y_zh = row_ids % row_count, row_ids // row_count % XS, row_ids // (row_count * XS)
    away = (lax.axis_index("x") + XS - x) % XS
    source = (away * (YS * ZHS) + (y_zh ^ lax.axis_index("zh"))) * row_count + i
    pick = (source[:, None] == row_ids[None, :]).astype(jnp.bfloat16)

    slabs_each = unit_count // EXPERT_COUNT
    expert_id = jnp.sum(jnp.where(own_row == place, unit_ids, 0), keepdims=True) // slabs_each
    kept, slab = hidden_units(expert_id, pick, own_rows, weights, True)
    (sent,) = hidden_units(expert_id, pick, other_rows, weights, False)
    received = lax.ppermute(sent, "c", [(0, 1), (1, 0)])
    chunks = pair_outputs(kept, received)
    chunks = lax.all_to_all(chunks, ("y", "zh", "x"), split_axis=0, concat_axis=0, tiled=True)
    decoded = sum_chunks(chunks)
    return (master_out, slab[None, None], decoded[None])


def solution(mesh):
    names = ("g",) + ALONG
    fine = Mesh(mesh.devices.reshape(GROUPS, YS, ZHS, XS, CORES), names)
    split = P("g", ALONG, None)
    return jax.shard_map(
        per_device,
        mesh=fine,
        in_specs=(split, split, split, split, P(), split, split, split),
        out_specs=(split, P("g", ALONG, None, None), split),
        check_vma=False,
    )
```

```python
import jax
import jax.numpy as jnp
from jax import lax
from jax.experimental import pallas as pl
from jax.experimental.pallas import tpu as pltpu
from jax.sharding import Mesh, PartitionSpec as P

adam_step = 1000.0
adam_eps = 1e-08
learn_rate = 0.005
weight_decay = 0.1
beta_one = 0.9
beta_two = 0.999

GROUPS, YS, ZHS, XS, CORES = 4, 8, 2, 4, 2
ALONG = ("y", "zh", "x", "c")
EXPERT_COUNT = 16
EXTRA = 128


def extend_rows(copies, tokens, routed, gates):
    _, row_count, depth = tokens.shape
    top = routed.shape[2]

    def kernel(tokens_ref, routed_ref, gates_ref, out_ref):
        lane = lax.broadcasted_iota(jnp.int32, (row_count, EXTRA), 1)
        expert = jnp.where(lane < EXPERT_COUNT, lane, lane - EXPERT_COUNT)
        routed_here, gates_here = routed_ref[0], gates_ref[0]
        coefficient = jnp.zeros((row_count, EXTRA), jnp.float32)
        for k in range(top):
            named = routed_here[:, k : k + 1] == expert
            coefficient += jnp.where(named, gates_here[:, k : k + 1], 0.0)
        high = coefficient.astype(jnp.bfloat16).astype(jnp.float32)
        extra = jnp.where(lane < EXPERT_COUNT, high, coefficient - high)
        extra = jnp.where(lane < 2 * EXPERT_COUNT, extra, 0.0).astype(jnp.bfloat16)
        for k in range(copies):
            out_ref[k, :, :depth] = tokens_ref[0]
            out_ref[k, :, depth:] = extra

    return pl.pallas_call(
        kernel,
        out_shape=jax.ShapeDtypeStruct((copies, row_count, depth + EXTRA), jnp.bfloat16),
        in_specs=[pl.BlockSpec(memory_space=pltpu.VMEM)] * 3,
        out_specs=pl.BlockSpec(memory_space=pltpu.VMEM),
    )(tokens, routed, gates)


def place_slabs(group, placement, parts):
    count, rows, cols = parts[0].shape
    total = count * len(parts)

    def kernel(group_ref, placement_ref, a, b, c, d, out_hbm, sem):
        own = group_ref[0]
        for k, ref in enumerate((a, b, c, d)):
            base = ((own + k) % len(parts)) * count

            def body(i, _, ref=ref, base=base):
                pltpu.make_async_copy(ref.at[i], out_hbm.at[placement_ref[own, base + i]], sem).start()
                return 0

            lax.fori_loop(0, count, body, 0, unroll=8)
        pltpu.make_async_copy(out_hbm, out_hbm, sem).wait()

    return pl.pallas_call(
        kernel,
        out_shape=jax.ShapeDtypeStruct((total, rows, cols), parts[0].dtype),
        in_specs=[pl.BlockSpec(memory_space=pltpu.SMEM)] * 2 + [pl.BlockSpec(memory_space=pltpu.VMEM)] * 4,
        out_specs=pl.BlockSpec(memory_space=pltpu.HBM),
        scratch_shapes=[pltpu.SemaphoreType.DMA],
        compiler_params=pltpu.CompilerParams(vmem_limit_bytes=16 * 2**20),
    )(group, placement, *parts)


def hidden_units(expert_id, pick, rows, weights, with_slab):
    half = rows.shape[0]
    depth = weights.shape[0]
    blocks = 4
    piece = depth // blocks

    def kernel(expert_ref, pick_ref, rows_ref, w_ref, out_ref, *slab):
        copies = []
        if with_slab:
            slab_hbm, sems = slab
            copies = [
                pltpu.make_async_copy(
                    w_ref.at[pl.ds(k * piece, piece)], slab_hbm.at[pl.ds(k * piece, piece)], sems.at[k]
                )
                for k in range(blocks)
            ]
        for copy in copies:
            copy.start()
        out_ref[half:, :] = w_ref[:, 256:]
        expert = expert_ref[0]
        lane = lax.broadcasted_iota(jnp.int32, (1, EXTRA), 1)
        own = jnp.where((lane == expert) | (lane == expert + EXPERT_COUNT), 1.0, 0.0)
        gate_up = jnp.dot(rows_ref[:, :depth], w_ref[:, :256], preferred_element_type=jnp.float32)
        gate, up = gate_up[:, :128], gate_up[:, 128:]
        hidden = (gate / (1.0 + jnp.exp(-gate)) * up).astype(jnp.bfloat16).astype(jnp.float32)
        extra = rows_ref[:, depth:].astype(jnp.float32)
        coefficient = jnp.sum(extra * own, axis=1, keepdims=True)
        scaled = (hidden * coefficient).astype(jnp.bfloat16)
        ordered = jnp.dot(pick_ref[...], scaled, preferred_element_type=jnp.float32)
        out_ref[:half, :] = ordered.astype(jnp.bfloat16)
        for copy in copies:
            copy.wait()

    out_shape = (jax.ShapeDtypeStruct((half + depth, 128), jnp.bfloat16),)
    out_specs = (pl.BlockSpec(memory_space=pltpu.VMEM),)
    if with_slab:
        out_shape += (jax.ShapeDtypeStruct(weights.shape, jnp.bfloat16),)
        out_specs += (pl.BlockSpec(memory_space=pltpu.HBM),)
    return pl.pallas_call(
        kernel,
        out_shape=out_shape,
        in_specs=[pl.BlockSpec(memory_space=pltpu.SMEM)] + [pl.BlockSpec(memory_space=pltpu.VMEM)] * 3,
        out_specs=out_specs,
        scratch_shapes=[pltpu.SemaphoreType.DMA((blocks,))] if with_slab else [],
        compiler_params=pltpu.CompilerParams(vmem_limit_bytes=24 * 2**20),
    )(expert_id, pick, rows, weights)


def pair_outputs(kept, received):
    chips = YS * ZHS * XS
    half = chips * 4
    depth = kept.shape[0] - half
    lanes = depth // 128

    def kernel(kept_ref, recv_ref, out_ref, part_ref):
        for k in range(4):
            span = slice(half + k * depth // 4, half + (k + 1) * depth // 4)
            part_ref[:, k * depth // 4 : (k + 1) * depth // 4] = sum(
                lax.dot_general(
                    ref[:half, :], ref[span, :], (((1,), (1,)), ((), ())), preferred_element_type=jnp.float32
                )
                for ref in (kept_ref, recv_ref)
            )
        low = lax.broadcasted_iota(jnp.int32, (chips // 2, 8, 128), 1) < 4

        def tile(q):
            return part_ref[:, q * 128 : (q + 1) * 128].reshape(chips // 2, 8, 128)

        for q in range(0, lanes, 4):
            first, second = [], []
            for p in (q, q + 2):
                a, b = tile(p), tile(p + 1)
                first.append(jnp.where(low, a, pltpu.roll(b, 4, 1)))
                second.append(jnp.where(low, pltpu.roll(a, 4, 1), b))
            out_ref[:, 0, 4 * q : 4 * q + 16, :] = jnp.concatenate(first, axis=1).astype(jnp.bfloat16)
            out_ref[:, 1, 4 * q : 4 * q + 16, :] = jnp.concatenate(second, axis=1).astype(jnp.bfloat16)

    out = pl.pallas_call(
        kernel,
        out_shape=jax.ShapeDtypeStruct((chips // 2, 2, 4 * lanes, 128), jnp.bfloat16),
        in_specs=[pl.BlockSpec(memory_space=pltpu.VMEM)] * 2,
        out_specs=pl.BlockSpec(memory_space=pltpu.VMEM),
        scratch_shapes=[pltpu.VMEM((half, depth), jnp.float32)],
        compiler_params=pltpu.CompilerParams(vmem_limit_bytes=24 * 2**20),
    )(kept, received)
    return out.reshape(chips, 4 * lanes, 128)


def sum_chunks(chunks):
    count, tall, _ = chunks.shape
    lanes = tall // 4

    def kernel(ref, out_ref):
        total = ref[0].astype(jnp.float32)
        for k in range(1, count):
            total += ref[k].astype(jnp.float32)
        out_ref[...] = jnp.concatenate(
            [total[4 * q : 4 * q + 4, :] for q in range(lanes)], axis=1
        ).astype(jnp.bfloat16)

    return pl.pallas_call(
        kernel,
        out_shape=jax.ShapeDtypeStruct((4, lanes * 128), jnp.bfloat16),
        in_specs=[pl.BlockSpec(memory_space=pltpu.VMEM)],
        out_specs=pl.BlockSpec(memory_space=pltpu.VMEM),
        compiler_params=pltpu.CompilerParams(vmem_limit_bytes=32 * 2**20),
    )(chunks)


def per_device(
    master_weights,
    first_moment,
    second_moment,
    gradient,
    placement,
    tokens,
    routed_expert_index,
    gate_weights,
):
    group = lax.axis_index("g")
    place = lax.axis_index(ALONG)
    row_count, depth = tokens.shape[1:]

    own_rows = extend_rows(1, tokens, routed_expert_index, gate_weights)[0]
    other_rows = lax.ppermute(own_rows, "zh", [(0, 1), (1, 0)])

    grad_float = gradient.astype(jnp.float32)
    first_new = beta_one * first_moment + (1.0 - beta_one) * grad_float
    second_new = beta_two * second_moment + (1.0 - beta_two) * grad_float * grad_float
    update = (
        first_new
        / (1.0 - beta_one**adam_step)
        / (jnp.sqrt(second_new / (1.0 - beta_two**adam_step)) + adam_eps)
    )
    master_out = master_weights - learn_rate * (update + weight_decay * master_weights)
    rounded = master_out.astype(jnp.bfloat16)
    other_rows, _ = lax.optimization_barrier((other_rows, rounded))

    parts = [rounded] + [
        lax.ppermute(rounded, "g", [((i + s) % GROUPS, i) for i in range(GROUPS)])
        for s in range(1, GROUPS)
    ]

    pair = jnp.concatenate([own_rows, other_rows], axis=0)
    column = lax.all_gather(pair, "y", axis=0, tiled=True)
    parts, column = lax.optimization_barrier((parts, column))

    others = [lax.ppermute(column, "x", [(k, (k + t) % XS) for k in range(XS)]) for t in (2, 1, 3)]
    own_rows = jnp.concatenate([column] + others, axis=0)
    other_rows = lax.ppermute(own_rows, "c", [(0, 1), (1, 0)])

    unit_count = placement.shape[1]
    unit_ids = jnp.arange(unit_count, dtype=jnp.int32)
    own_row = lax.dynamic_index_in_dim(placement, group, 0, keepdims=False)
    ordered = place_slabs(jnp.full((1,), group, jnp.int32), placement, parts)
    own_slab = lax.all_to_all(ordered, ALONG, split_axis=0, concat_axis=0, tiled=True)
    weights = own_slab.reshape(depth, -1)

    row_ids = jnp.arange(own_rows.shape[0], dtype=jnp.int32)
    i, x, y_zh = row_ids % row_count, row_ids // row_count % XS, row_ids // (row_count * XS)
    away = (lax.axis_index("x") + XS - x) % XS
    away = jnp.where(away == 1, 2, jnp.where(away == 2, 1, away))
    source = (away * (YS * ZHS) + (y_zh ^ lax.axis_index("zh"))) * row_count + i
    pick = (source[:, None] == row_ids[None, :]).astype(jnp.bfloat16)

    slabs_each = unit_count // EXPERT_COUNT
    expert_id = jnp.sum(jnp.where(own_row == place, unit_ids, 0), keepdims=True) // slabs_each
    kept, slab = hidden_units(expert_id, pick, own_rows, weights, True)
    (sent,) = hidden_units(expert_id, pick, other_rows, weights, False)
    received = lax.ppermute(sent, "c", [(0, 1), (1, 0)])
    chunks = pair_outputs(kept, received)
    chunks = lax.all_to_all(chunks, ("y", "zh", "x"), split_axis=0, concat_axis=0, tiled=True)
    decoded = sum_chunks(chunks)
    return (master_out, slab[None, None], decoded[None])


def solution(mesh):
    names = ("g",) + ALONG
    fine = Mesh(mesh.devices.reshape(GROUPS, YS, ZHS, XS, CORES), names)
    split = P("g", ALONG, None)
    return jax.shard_map(
        per_device,
        mesh=fine,
        in_specs=(split, split, split, split, P(), split, split, split),
        out_specs=(split, P("g", ALONG, None, None), split),
        check_vma=False,
    )
```

```python
import jax
import jax.numpy as jnp
from jax import lax
from jax.experimental import pallas as pl
from jax.experimental.pallas import tpu as pltpu
from jax.sharding import Mesh, PartitionSpec as P

adam_step = 1000.0
adam_eps = 1e-08
learn_rate = 0.005
weight_decay = 0.1
beta_one = 0.9
beta_two = 0.999

GROUPS, YS, ZHS, XS, CORES = 4, 8, 2, 4, 2
ALONG = ("y", "zh", "x", "c")
EXPERT_COUNT = 16
EXTRA = 128
RELAY = (1, 3, 2)


def extend_rows(copies, tokens, routed, gates):
    _, row_count, depth = tokens.shape
    top = routed.shape[2]

    def kernel(tokens_ref, routed_ref, gates_ref, out_ref):
        lane = lax.broadcasted_iota(jnp.int32, (row_count, EXTRA), 1)
        expert = jnp.where(lane < EXPERT_COUNT, lane, lane - EXPERT_COUNT)
        routed_here, gates_here = routed_ref[0], gates_ref[0]
        coefficient = jnp.zeros((row_count, EXTRA), jnp.float32)
        for k in range(top):
            named = routed_here[:, k : k + 1] == expert
            coefficient += jnp.where(named, gates_here[:, k : k + 1], 0.0)
        high = coefficient.astype(jnp.bfloat16).astype(jnp.float32)
        extra = jnp.where(lane < EXPERT_COUNT, high, coefficient - high)
        extra = jnp.where(lane < 2 * EXPERT_COUNT, extra, 0.0).astype(jnp.bfloat16)
        for k in range(copies):
            out_ref[k, :, :depth] = tokens_ref[0]
            out_ref[k, :, depth:] = extra

    return pl.pallas_call(
        kernel,
        out_shape=jax.ShapeDtypeStruct((copies, row_count, depth + EXTRA), jnp.bfloat16),
        in_specs=[pl.BlockSpec(memory_space=pltpu.VMEM)] * 3,
        out_specs=pl.BlockSpec(memory_space=pltpu.VMEM),
    )(tokens, routed, gates)


def place_slabs(group, placement, parts):
    count, rows, cols = parts[0].shape
    total = count * len(parts)

    def kernel(group_ref, placement_ref, a, b, c, d, out_hbm, sem):
        own = group_ref[0]
        for k, ref in enumerate((a, b, c, d)):
            base = ((own + (0, *RELAY)[k]) % len(parts)) * count

            def body(i, _, ref=ref, base=base):
                pltpu.make_async_copy(ref.at[i], out_hbm.at[placement_ref[own, base + i]], sem).start()
                return 0

            lax.fori_loop(0, count, body, 0, unroll=8)
        pltpu.make_async_copy(out_hbm, out_hbm, sem).wait()

    return pl.pallas_call(
        kernel,
        out_shape=jax.ShapeDtypeStruct((total, rows, cols), parts[0].dtype),
        in_specs=[pl.BlockSpec(memory_space=pltpu.SMEM)] * 2 + [pl.BlockSpec(memory_space=pltpu.VMEM)] * 4,
        out_specs=pl.BlockSpec(memory_space=pltpu.HBM),
        scratch_shapes=[pltpu.SemaphoreType.DMA],
        compiler_params=pltpu.CompilerParams(vmem_limit_bytes=16 * 2**20),
    )(group, placement, *parts)


def hidden_units(expert_id, pick, rows, weights, with_slab):
    half = rows.shape[0]
    depth = weights.shape[0]
    blocks = 4
    piece = depth // blocks

    def kernel(expert_ref, pick_ref, rows_ref, w_ref, out_ref, *slab):
        copies = []
        if with_slab:
            slab_hbm, sems = slab
            copies = [
                pltpu.make_async_copy(
                    w_ref.at[pl.ds(k * piece, piece)], slab_hbm.at[pl.ds(k * piece, piece)], sems.at[k]
                )
                for k in range(blocks)
            ]
        for copy in copies:
            copy.start()
        out_ref[half:, :] = w_ref[:, 256:]
        expert = expert_ref[0]
        lane = lax.broadcasted_iota(jnp.int32, (1, EXTRA), 1)
        own = jnp.where((lane == expert) | (lane == expert + EXPERT_COUNT), 1.0, 0.0)
        gate_up = jnp.dot(rows_ref[:, :depth], w_ref[:, :256], preferred_element_type=jnp.float32)
        gate, up = gate_up[:, :128], gate_up[:, 128:]
        hidden = (gate / (1.0 + jnp.exp(-gate)) * up).astype(jnp.bfloat16).astype(jnp.float32)
        extra = rows_ref[:, depth:].astype(jnp.float32)
        coefficient = jnp.sum(extra * own, axis=1, keepdims=True)
        scaled = (hidden * coefficient).astype(jnp.bfloat16)
        ordered = jnp.dot(pick_ref[...], scaled, preferred_element_type=jnp.float32)
        out_ref[:half, :] = ordered.astype(jnp.bfloat16)
        for copy in copies:
            copy.wait()

    out_shape = (jax.ShapeDtypeStruct((half + depth, 128), jnp.bfloat16),)
    out_specs = (pl.BlockSpec(memory_space=pltpu.VMEM),)
    if with_slab:
        out_shape += (jax.ShapeDtypeStruct(weights.shape, jnp.bfloat16),)
        out_specs += (pl.BlockSpec(memory_space=pltpu.HBM),)
    return pl.pallas_call(
        kernel,
        out_shape=out_shape,
        in_specs=[pl.BlockSpec(memory_space=pltpu.SMEM)] + [pl.BlockSpec(memory_space=pltpu.VMEM)] * 3,
        out_specs=out_specs,
        scratch_shapes=[pltpu.SemaphoreType.DMA((blocks,))] if with_slab else [],
        compiler_params=pltpu.CompilerParams(vmem_limit_bytes=24 * 2**20),
    )(expert_id, pick, rows, weights)


def pair_outputs(kept, received):
    chips = YS * ZHS * XS
    half = chips * 4
    depth = kept.shape[0] - half
    lanes = depth // 128

    def kernel(kept_ref, recv_ref, out_ref, part_ref):
        for k in range(4):
            span = slice(half + k * depth // 4, half + (k + 1) * depth // 4)
            part_ref[:, k * depth // 4 : (k + 1) * depth // 4] = sum(
                lax.dot_general(
                    ref[:half, :], ref[span, :], (((1,), (1,)), ((), ())), preferred_element_type=jnp.float32
                )
                for ref in (kept_ref, recv_ref)
            )
        low = lax.broadcasted_iota(jnp.int32, (chips // 2, 8, 128), 1) < 4

        def tile(q):
            return part_ref[:, q * 128 : (q + 1) * 128].reshape(chips // 2, 8, 128)

        for q in range(0, lanes, 4):
            first, second = [], []
            for p in (q, q + 2):
                a, b = tile(p), tile(p + 1)
                first.append(jnp.where(low, a, pltpu.roll(b, 4, 1)))
                second.append(jnp.where(low, pltpu.roll(a, 4, 1), b))
            out_ref[:, 0, 4 * q : 4 * q + 16, :] = jnp.concatenate(first, axis=1).astype(jnp.bfloat16)
            out_ref[:, 1, 4 * q : 4 * q + 16, :] = jnp.concatenate(second, axis=1).astype(jnp.bfloat16)

    out = pl.pallas_call(
        kernel,
        out_shape=jax.ShapeDtypeStruct((chips // 2, 2, 4 * lanes, 128), jnp.bfloat16),
        in_specs=[pl.BlockSpec(memory_space=pltpu.VMEM)] * 2,
        out_specs=pl.BlockSpec(memory_space=pltpu.VMEM),
        scratch_shapes=[pltpu.VMEM((half, depth), jnp.float32)],
        compiler_params=pltpu.CompilerParams(vmem_limit_bytes=24 * 2**20),
    )(kept, received)
    return out.reshape(chips, 4 * lanes, 128)


def sum_chunks(chunks):
    count, tall, _ = chunks.shape
    lanes = tall // 4

    def kernel(ref, out_ref):
        total = ref[0].astype(jnp.float32)
        for k in range(1, count):
            total += ref[k].astype(jnp.float32)
        out_ref[...] = jnp.concatenate(
            [total[4 * q : 4 * q + 4, :] for q in range(lanes)], axis=1
        ).astype(jnp.bfloat16)

    return pl.pallas_call(
        kernel,
        out_shape=jax.ShapeDtypeStruct((4, lanes * 128), jnp.bfloat16),
        in_specs=[pl.BlockSpec(memory_space=pltpu.VMEM)],
        out_specs=pl.BlockSpec(memory_space=pltpu.VMEM),
        compiler_params=pltpu.CompilerParams(vmem_limit_bytes=32 * 2**20),
    )(chunks)


def per_device(
    master_weights,
    first_moment,
    second_moment,
    gradient,
    placement,
    tokens,
    routed_expert_index,
    gate_weights,
):
    group = lax.axis_index("g")
    place = lax.axis_index(ALONG)
    row_count, depth = tokens.shape[1:]

    own_rows = extend_rows(1, tokens, routed_expert_index, gate_weights)[0]
    other_rows = lax.ppermute(own_rows, "zh", [(0, 1), (1, 0)])

    grad_float = gradient.astype(jnp.float32)
    first_new = beta_one * first_moment + (1.0 - beta_one) * grad_float
    second_new = beta_two * second_moment + (1.0 - beta_two) * grad_float * grad_float
    update = (
        first_new
        / (1.0 - beta_one**adam_step)
        / (jnp.sqrt(second_new / (1.0 - beta_two**adam_step)) + adam_eps)
    )
    master_out = master_weights - learn_rate * (update + weight_decay * master_weights)
    rounded = master_out.astype(jnp.bfloat16)
    other_rows, _ = lax.optimization_barrier((other_rows, rounded))

    parts = [rounded] + [
        lax.ppermute(rounded, "g", [((i + s) % GROUPS, i) for i in range(GROUPS)])
        for s in RELAY
    ]

    pair = jnp.concatenate([own_rows, other_rows], axis=0)
    column = lax.all_gather(pair, "y", axis=0, tiled=True)
    parts, column = lax.optimization_barrier((parts, column))

    others = [lax.ppermute(column, "x", [(k, (k + t) % XS) for k in range(XS)]) for t in (2, 1, 3)]
    own_rows = jnp.concatenate([column] + others, axis=0)
    other_rows = lax.ppermute(own_rows, "c", [(0, 1), (1, 0)])

    unit_count = placement.shape[1]
    unit_ids = jnp.arange(unit_count, dtype=jnp.int32)
    own_row = lax.dynamic_index_in_dim(placement, group, 0, keepdims=False)
    ordered = place_slabs(jnp.full((1,), group, jnp.int32), placement, parts)
    own_slab = lax.all_to_all(ordered, ALONG, split_axis=0, concat_axis=0, tiled=True)
    weights = own_slab.reshape(depth, -1)

    row_ids = jnp.arange(own_rows.shape[0], dtype=jnp.int32)
    i, x, y_zh = row_ids % row_count, row_ids // row_count % XS, row_ids // (row_count * XS)
    away = (lax.axis_index("x") + XS - x) % XS
    away = jnp.where(away == 1, 2, jnp.where(away == 2, 1, away))
    source = (away * (YS * ZHS) + (y_zh ^ lax.axis_index("zh"))) * row_count + i
    pick = (source[:, None] == row_ids[None, :]).astype(jnp.bfloat16)

    slabs_each = unit_count // EXPERT_COUNT
    expert_id = jnp.sum(jnp.where(own_row == place, unit_ids, 0), keepdims=True) // slabs_each
    kept, slab = hidden_units(expert_id, pick, own_rows, weights, True)
    (sent,) = hidden_units(expert_id, pick, other_rows, weights, False)
    received = lax.ppermute(sent, "c", [(0, 1), (1, 0)])
    chunks = pair_outputs(kept, received)
    chunks = lax.all_to_all(chunks, ("y", "zh", "x"), split_axis=0, concat_axis=0, tiled=True)
    decoded = sum_chunks(chunks)
    return (master_out, slab[None, None], decoded[None])


def solution(mesh):
    names = ("g",) + ALONG
    fine = Mesh(mesh.devices.reshape(GROUPS, YS, ZHS, XS, CORES), names)
    split = P("g", ALONG, None)
    return jax.shard_map(
        per_device,
        mesh=fine,
        in_specs=(split, split, split, split, P(), split, split, split),
        out_specs=(split, P("g", ALONG, None, None), split),
        check_vma=False,
    )
```
